512 devices in a mesh: dp: 64 (over x, y_lo, z), vocab: 8 (over y_hi, core).
Axes of the slice: x: 4, y: 8 (y_hi: 4, y_lo: 2; y = y_hi * 2 + y_lo), z: 8, core: 2. Of those that a mesh axis runs over, the one named last changes fastest.
Arguments:
- hidden: bfloat16 [32768, 4096], P(('dp', 'vocab')), may hold values from -64 to 64
- targets: int32 [32768], P('dp'), may hold values from 0 to 1535
- token_weight: float32 [32768], P('dp'), may hold values from 0.25 to 4
- head_weight: bfloat16 [1536, 4096], P('vocab')
Outputs:
- token_loss: float32 [32768], P(('dp', 'vocab'))
- grad_hidden: bfloat16 [32768, 4096], P(('dp', 'vocab'))
- grad_weight: bfloat16 [1536, 4096], P('vocab')
The draws below stay inside these ranges and needn't reach their ends.
All inputs are finite; a program needn't handle non-finite values.
Results may differ from the reference program's by a relative error of at most 0.012.
Values may be sent and summed in bfloat16 or wider, within the bound.
No kernel may reach another device: no remote copies, remote signals or barrier semaphores. Data moves between devices by JAX's collectives and lax.ppermute only.
A program may use at most 64 MiB of HBM per device.

```python
import math
import jax
import jax.numpy as jnp
from jax import lax

D = 4096
V_DEV = 192
TOK_DEV = 64
VOCAB = 1536
TOKENS = 32768
N_VOCAB = 8


def shared_head(key):
    gaussian = jax.random.normal(jax.random.fold_in(key, 11), (VOCAB, D), jnp.float32)
    spread = jnp.exp(jax.random.uniform(jax.random.fold_in(key, 12), (VOCAB, 1), jnp.float32, math.log(0.6), math.log(1.6)))
    rising = 0.5 + jnp.arange(VOCAB, dtype=jnp.float32)[:, None] / VOCAB
    return (gaussian, spread * rising)


def head_rows(gaussian, scales):
    return (jnp.clip(gaussian, -4.0, 4.0) * scales * (3.0 / math.sqrt(D))).astype(jnp.bfloat16)


def draw_head_weight(key, part):
    gaussian, scales = shared_head(key)
    return head_rows(gaussian, scales)


def draw_hidden(key, part):
    own_key = jax.random.fold_in(key, 2)
    scale_key = jax.random.fold_in(own_key, 1)
    bulk_key = jax.random.fold_in(own_key, 2)
    ground = jnp.clip(jax.random.normal(bulk_key, (TOKENS, D), jnp.float32), -4.0, 4.0)
    row_scale = jnp.exp(jax.random.uniform(scale_key, (TOKENS, 1), jnp.float32, math.log(0.4), math.log(4.0)))
    result = ground * row_scale
    return result.astype(jnp.bfloat16)


def set_ends(values, rng, least, top_value):
    shape = values.shape
    index_at = [jax.random.randint(jax.random.fold_in(rng, axis), (), 0, shape[axis]) for axis in range(len(shape))]
    values = values.at[tuple(index_at)].set(least)
    longest = shape.index(max(shape))
    index_at[longest] = (index_at[longest] + 1) % shape[longest]
    return values.at[tuple(index_at)].set(top_value)


def shard_levels(rng, dims, cuts, least, top_value):
    level = 1.0
    for position, shards_of in cuts:
        draws = jax.random.uniform(jax.random.fold_in(jax.random.fold_in(rng, 6), position), (shards_of,), jnp.float32, least / len(cuts), top_value / len(cuts))
        level = level * jnp.repeat(jnp.exp(draws), dims[position] // shards_of).reshape((-1,) + (1,) * (len(dims) - 1 - position))
    return level


def setup_inputs(seed: int = 0) -> dict:
    keys = jax.random.split(jax.random.key(seed), 5)
    hidden = draw_hidden(jax.random.fold_in(keys[4], 71), 0)
    targets = set_ends(jax.random.randint(keys[1], (TOKENS,), 0, VOCAB), jax.random.fold_in(keys[1], 1), 0, VOCAB - 1).astype(jnp.int32)
    token_weight = jnp.clip(jnp.exp(math.log(4.0) - 2.7725887 * jax.random.uniform(keys[2], (TOKENS,), jnp.float32) ** shard_levels(keys[2], (TOKENS,), ((0, 64),), -0.2, 0.2)), 0.25, 4.0)
    head_weight = draw_head_weight(jax.random.fold_in(keys[4], 71), 0)
    return {"hidden": hidden, "targets": targets, "token_weight": token_weight, "head_weight": head_weight}


def reference(hidden, targets, token_weight, head_weight):
    group_rows = TOK_DEV * N_VOCAB
    groups = TOKENS // group_rows
    hidden_blocks = hidden.reshape(groups, group_rows, D)
    target_blocks = targets.reshape(groups, group_rows)
    weight_blocks = token_weight.reshape(groups, group_rows)
    stacked_head = head_weight.reshape(N_VOCAB, V_DEV, D).astype(jnp.float32)
    columns = jnp.arange(VOCAB, dtype=jnp.int32)[None, :]

    def block_step(weight_acc, batch_items):
        segment, labels, row_weight = batch_items
        logits = jnp.dot(segment, head_weight.T, preferred_element_type=jnp.float32)
        row_top = jnp.max(logits, axis=1)
        log_total = row_top + jnp.log(jnp.sum(jnp.exp(logits - row_top[:, None]), axis=1))
        target_hit = columns == labels[:, None]
        target_logit = jnp.sum(jnp.where(target_hit, logits, jnp.zeros_like(logits)), axis=1)
        row_loss = log_total - target_logit
        softmax_rows = jnp.exp(logits - log_total[:, None])
        score_grad = (row_weight[:, None] * (softmax_rows - target_hit.astype(jnp.float32))).astype(jnp.bfloat16)
        shard_terms = jnp.einsum("rjv,jvd->rjd", score_grad.reshape(group_rows, N_VOCAB, V_DEV).astype(jnp.float32), stacked_head)
        rounded = lax.optimization_barrier(shard_terms.astype(jnp.bfloat16)).astype(jnp.float32)
        grad_rows = jnp.sum(rounded, axis=1).astype(jnp.bfloat16)
        weight_acc = weight_acc + jnp.dot(score_grad.T, segment, preferred_element_type=jnp.float32)
        return weight_acc, (row_loss, grad_rows)

    weight_acc, outputs = lax.scan(block_step, jnp.zeros((VOCAB, D), jnp.float32), (hidden_blocks, target_blocks, weight_blocks))
    token_loss = outputs[0].reshape(TOKENS)
    grad_hidden = outputs[1].reshape(TOKENS, D)
    return token_loss, grad_hidden, weight_acc.astype(jnp.bfloat16)
```

```python
import jax
import jax.numpy as jnp
from jax import lax
from jax.sharding import Mesh
from jax.sharding import PartitionSpec as P

F32, BF16 = jnp.float32, jnp.bfloat16
DP = ("x", "yl", "z")


def shift(value, axis, step, size):
    return lax.ppermute(value, axis, [(i, (i + step) % size) for i in range(size)])


def relative(value, yh, core):
    n_yh, n_core, _ = value.shape
    value = lax.dynamic_slice_in_dim(jnp.concatenate([value, value], 0), yh, n_yh, 0)
    value = lax.dynamic_slice_in_dim(jnp.concatenate([value, value], 1), core, n_core, 1)
    return value.transpose(1, 0, 2).reshape(-1)


def merge(a, b):
    top = jnp.maximum(a[0], b[0])
    return jnp.stack([top, a[1] * jnp.exp(a[0] - top) + b[1] * jnp.exp(b[0] - top), a[2] + b[2]])


def per_device(hidden, targets, token_weight, head_weight, *, n_yh, n_dp):
    yh, core = lax.axis_index("yh"), lax.axis_index("core")
    tok, width = hidden.shape
    v_dev = head_weight.shape[0]
    half = tok // 2
    labels = relative(targets.reshape(n_yh, 2, tok), yh, core)
    weights = relative(token_weight.reshape(n_yh, 2, tok), yh, core)

    swap = lambda v: shift(v, "core", 1, 2)
    before = shift(hidden, "yh", 1, n_yh)
    after = shift(hidden, "yh", -1, n_yh)
    far_a = shift(before[:half], "yh", 1, n_yh)
    far_b = shift(after[half:], "yh", -1, n_yh)
    mine = [hidden, after, far_a, far_b, before]
    gathered = jnp.concatenate(mine + [swap(v) for v in mine], 0)

    logits = lax.dot_general(gathered, head_weight, (((1,), (1,)), ((), ())), preferred_element_type=F32)
    columns = (yh * 2 + core) * v_dev + lax.broadcasted_iota(jnp.int32, (1, v_dev), 1)
    hit = columns == labels[:, None]
    top = jnp.max(logits, axis=1)
    total = jnp.sum(jnp.exp(logits - top[:, None]), axis=1)
    target = jnp.sum(jnp.where(hit, logits, jnp.zeros_like(logits)), axis=1)
    stats = jnp.stack([top, total, target]).reshape(3, 2, n_yh, tok)
    stats = merge(stats, swap(stats)[:, ::-1])
    others = [jnp.roll(shift(stats, "yh", s, n_yh), -s, axis=2) for s in (1, 2, 3)]
    stats = merge(merge(stats, others[0]), merge(others[1], others[2])).reshape(3, -1)
    log_total = stats[0] + jnp.log(stats[1])
    token_loss = (log_total - stats[2])[:tok]

    softmax = jnp.exp(logits - log_total[:, None])
    score = (weights[:, None] * (softmax - hit.astype(F32))).astype(BF16)

    partial = lax.dot_general(score, gathered, (((0,), (0,)), ((), ())), preferred_element_type=F32).astype(BF16)
    rows, cols = v_dev // 4, width * 4 // n_dp
    chunks = partial.reshape(4, rows, n_dp // 4, cols).transpose(0, 2, 1, 3).reshape(n_dp, rows, cols)
    chunks = lax.all_to_all(chunks, DP, 0, 0, tiled=True)

    terms = jnp.dot(score, head_weight, preferred_element_type=F32).astype(BF16)
    own = n_yh * tok
    terms = (terms[:own].astype(F32) + swap(terms[own:]).astype(F32)).astype(BF16).reshape(n_yh, tok, width)
    grad_hidden = terms[0].astype(F32)
    for s in range(1, n_yh):
        grad_hidden = grad_hidden + shift(terms[s], "yh", s, n_yh).astype(F32)
    grad_hidden = grad_hidden.astype(BF16)

    chunk = jnp.sum(chunks.astype(F32), axis=0).astype(BF16)
    chunks = lax.all_to_all(jnp.broadcast_to(chunk, (n_dp, rows, cols)), DP, 0, 0, tiled=True)
    grad_weight = chunks.reshape(4, n_dp // 4, rows, cols).transpose(0, 2, 1, 3).reshape(v_dev, width)
    return token_loss, grad_hidden, grad_weight


def fine(mesh_devices, sizes):
    mesh = Mesh(mesh_devices.reshape(sizes), ("x", "yl", "z", "yh", "core"))

    def body(*args):
        return per_device(*args, n_yh=sizes[3], n_dp=sizes[0] * sizes[1] * sizes[2])

    tokens = ("x", "yl", "z", "yh", "core")
    return jax.shard_map(
        body,
        mesh=mesh,
        in_specs=(P(tokens, None), P(DP), P(DP), P(("yh", "core"), None)),
        out_specs=(P(tokens), P(tokens, None), P(("yh", "core"), None)),
        check_vma=False,
    )


def solution(mesh):
    return fine(mesh.devices, (4, 2, 8, 4, 2))
```

```python
import jax
import jax.numpy as jnp
from jax import lax
from jax.sharding import Mesh
from jax.sharding import PartitionSpec as P

F32, BF16 = jnp.float32, jnp.bfloat16
DP = ("x", "yl", "z")
VOCAB = ("yh", "core")


def shift(value, axis, step, size):
    return lax.ppermute(value, axis, [(i, (i + step) % size) for i in range(size)])


def swap(value):
    return shift(value, "core", 1, 2)


def by_core(value, core):
    return jnp.where(core == 0, value, value[::-1])


def gather_yh(hidden, yh, n_yh):
    half = hidden.shape[0] // 2
    low, high = hidden[:half], hidden[half:]
    up_low = shift(low, "yh", 1, n_yh)
    down_high = shift(high, "yh", -1, n_yh)
    up_high = shift(high, "yh", 1, n_yh)
    down_low = shift(low, "yh", -1, n_yh)
    far_low = shift(up_low, "yh", 1, n_yh)
    far_high = shift(down_high, "yh", -1, n_yh)
    out = jnp.zeros((n_yh, 2, half, hidden.shape[1]), hidden.dtype)
    out = lax.dynamic_update_slice(out, hidden.reshape(1, 2, half, -1), (yh, 0, 0, 0))
    before, after, far = (yh - 1) % n_yh, (yh + 1) % n_yh, (yh + 2) % n_yh
    for piece, owner, part in (
        (up_low, before, 0),
        (down_high, after, 1),
        (up_high, before, 1),
        (down_low, after, 0),
        (far_low, far, 0),
        (far_high, far, 1),
    ):
        out = lax.dynamic_update_slice(out, piece[None, None], (owner, part, 0, 0))
    return out.reshape(n_yh * 2 * half, -1)


def per_device(hidden, targets, token_weight, head_weight, *, n_yh, n_dp):
    yh, core = lax.axis_index("yh"), lax.axis_index("core")
    tok, width = hidden.shape
    v_dev = head_weight.shape[0]
    n_own = n_yh * tok
    rows_t, rows_v = (((1,), (1,)), ((), ())), (((0,), (0,)), ((), ()))
    labels = by_core(targets.reshape(n_yh, 2, tok).transpose(1, 0, 2), core).reshape(2, n_own)
    weights = by_core(token_weight.reshape(n_yh, 2, tok).transpose(1, 0, 2), core).reshape(2, n_own)

    own = gather_yh(hidden, yh, n_yh)
    gathered = (own, swap(own))

    columns = (yh * 2 + core) * v_dev + lax.broadcasted_iota(jnp.int32, (1, v_dev), 1)
    logits, hits, stats = [], [], []
    for k in range(2):
        part = lax.dot_general(gathered[k], head_weight, rows_t, preferred_element_type=F32)
        hit = columns == labels[k][:, None]
        top = jnp.max(part, axis=1)
        total = jnp.sum(jnp.exp(part - top[:, None]), axis=1)
        target = jnp.sum(jnp.where(hit, part, jnp.zeros_like(part)), axis=1)
        logits.append(part)
        hits.append(hit)
        stats.append(jnp.stack([top, total, target]))
    stats = by_core(jnp.stack(stats), core)
    stats = lax.all_to_all(jnp.broadcast_to(stats, (2 * n_yh,) + stats.shape), VOCAB, 0, 0, tiled=True)
    top = jnp.max(stats[:, :, 0], axis=0)
    log_total = top + jnp.log(jnp.sum(stats[:, :, 1] * jnp.exp(stats[:, :, 0] - top), axis=0))
    loss = by_core(log_total - jnp.sum(stats[:, :, 2], axis=0), core)[0]
    token_loss = lax.dynamic_slice_in_dim(loss, yh * tok, tok)
    log_total = by_core(log_total, core)

    score = [
        (weights[k][:, None] * (jnp.exp(logits[k] - log_total[k][:, None]) - hits[k].astype(F32))).astype(BF16)
        for k in range(2)
    ]

    away = jnp.dot(score[1], head_weight, preferred_element_type=F32).astype(BF16)
    home = jnp.dot(score[0], head_weight, preferred_element_type=F32).astype(BF16)
    terms = (home.astype(F32) + swap(away).astype(F32)).astype(BF16).reshape(n_yh, tok, width)

    partial = sum(lax.dot_general(score[k], gathered[k], rows_v, preferred_element_type=F32) for k in range(2))
    rows, cols = v_dev // 4, width * 4 // n_dp
    chunks = partial.astype(BF16).reshape(4, rows, n_dp // 4, cols).transpose(0, 2, 1, 3).reshape(n_dp, rows, cols)
    chunks, terms = lax.optimization_barrier((chunks, terms))
    chunks = lax.all_to_all(chunks, DP, 0, 0, tiled=True)

    grad_hidden = lax.dynamic_index_in_dim(terms, yh, 0, False).astype(F32)
    for s in (1, -1, 2):
        there = lax.dynamic_index_in_dim(terms, (yh + s) % n_yh, 0, False)
        grad_hidden = grad_hidden + shift(there, "yh", s, n_yh).astype(F32)
    grad_hidden = grad_hidden.astype(BF16)

    chunk = jnp.sum(chunks.astype(F32), axis=0).astype(BF16)
    chunks = lax.all_to_all(jnp.broadcast_to(chunk, (n_dp, rows, cols)), DP, 0, 0, tiled=True)
    grad_weight = chunks.reshape(4, n_dp // 4, rows, cols).transpose(0, 2, 1, 3).reshape(v_dev, width)
    return token_loss, grad_hidden, grad_weight


def fine(mesh_devices, sizes):
    mesh = Mesh(mesh_devices.reshape(sizes), ("x", "yl", "z", "yh", "core"))

    def body(*args):
        return per_device(*args, n_yh=sizes[3], n_dp=sizes[0] * sizes[1] * sizes[2])

    tokens = ("x", "yl", "z", "yh", "core")
    return jax.shard_map(
        body,
        mesh=mesh,
        in_specs=(P(tokens, None), P(DP), P(DP), P(VOCAB, None)),
        out_specs=(P(tokens), P(tokens, None), P(VOCAB, None)),
        check_vma=False,
    )


def solution(mesh):
    return fine(mesh.devices, (4, 2, 8, 4, 2))
```

```python
import jax
import jax.numpy as jnp
from jax import lax
from jax.sharding import Mesh
from jax.sharding import PartitionSpec as P

F32, BF16 = jnp.float32, jnp.bfloat16
DP = ("x", "yl", "z")
VOCAB = ("yh", "core")


def shift(value, axis, step, size):
    return lax.ppermute(value, axis, [(i, (i + step) % size) for i in range(size)])


def swap(value):
    return shift(value, "core", 1, 2)


def by_core(value, core):
    return jnp.where(core == 0, value, value[::-1])


def gather_yh(hidden, yh, n_yh):
    half = hidden.shape[0] // 2
    low, high = hidden[:half], hidden[half:]
    up_low = shift(low, "yh", 1, n_yh)
    down_high = shift(high, "yh", -1, n_yh)
    up_high = shift(high, "yh", 1, n_yh)
    down_low = shift(low, "yh", -1, n_yh)
    far_low = shift(up_low, "yh", 1, n_yh)
    far_high = shift(down_high, "yh", -1, n_yh)
    out = jnp.zeros((n_yh, 2, half, hidden.shape[1]), hidden.dtype)
    out = lax.dynamic_update_slice(out, hidden.reshape(1, 2, half, -1), (yh, 0, 0, 0))
    before, after, far = (yh - 1) % n_yh, (yh + 1) % n_yh, (yh + 2) % n_yh
    for piece, owner, part in (
        (up_low, before, 0),
        (down_high, after, 1),
        (up_high, before, 1),
        (down_low, after, 0),
        (far_low, far, 0),
        (far_high, far, 1),
    ):
        out = lax.dynamic_update_slice(out, piece[None, None], (owner, part, 0, 0))
    return out.reshape(n_yh * 2 * half, -1)


def per_device(hidden, targets, token_weight, head_weight, *, n_x, n_yl, n_z, n_yh):
    yh, core = lax.axis_index("yh"), lax.axis_index("core")
    tok, width = hidden.shape
    v_dev = head_weight.shape[0]
    n_own = n_yh * tok
    rows_t, rows_v = (((1,), (1,)), ((), ())), (((0,), (0,)), ((), ()))
    labels = by_core(targets.reshape(n_yh, 2, tok).transpose(1, 0, 2), core).reshape(2, n_own)
    weights = by_core(token_weight.reshape(n_yh, 2, tok).transpose(1, 0, 2), core).reshape(2, n_own)

    own = gather_yh(hidden, yh, n_yh)
    gathered = (own, swap(own))

    columns = (yh * 2 + core) * v_dev + lax.broadcasted_iota(jnp.int32, (1, v_dev), 1)
    logits, hits, stats = [], [], []
    for k in range(2):
        part = lax.dot_general(gathered[k], head_weight, rows_t, preferred_element_type=F32)
        hit = columns == labels[k][:, None]
        top = jnp.max(part, axis=1)
        total = jnp.sum(jnp.exp(part - top[:, None]), axis=1)
        target = jnp.sum(jnp.where(hit, part, jnp.zeros_like(part)), axis=1)
        logits.append(part)
        hits.append(hit)
        stats.append(jnp.stack([top, total, target]))
    stats = by_core(jnp.stack(stats), core)
    stats = lax.all_to_all(jnp.broadcast_to(stats, (2 * n_yh,) + stats.shape), VOCAB, 0, 0, tiled=True)
    top = jnp.max(stats[:, :, 0], axis=0)
    log_total = top + jnp.log(jnp.sum(stats[:, :, 1] * jnp.exp(stats[:, :, 0] - top), axis=0))
    loss = by_core(log_total - jnp.sum(stats[:, :, 2], axis=0), core)[0]
    token_loss = lax.dynamic_slice_in_dim(loss, yh * tok, tok)
    log_total = by_core(log_total, core)

    score = [
        (weights[k][:, None] * (jnp.exp(logits[k] - log_total[k][:, None]) - hits[k].astype(F32))).astype(BF16)
        for k in range(2)
    ]

    away = jnp.dot(score[1], head_weight, preferred_element_type=F32).astype(BF16)
    home = jnp.dot(score[0], head_weight, preferred_element_type=F32).astype(BF16)
    terms = (home.astype(F32) + swap(away).astype(F32)).astype(BF16).reshape(n_yh, tok, width)

    partial = sum(lax.dot_general(score[k], gathered[k], rows_v, preferred_element_type=F32) for k in range(2))
    part = partial.astype(BF16).reshape(n_x, v_dev // n_x, width)
    part = lax.all_to_all(part, "x", 0, 0, tiled=True)
    part = jnp.sum(part.astype(F32), axis=0).astype(BF16)
    part = part.reshape(v_dev // n_x, n_yl * n_z, -1).transpose(1, 0, 2)
    block = lambda s: lax.dynamic_index_in_dim(terms, (yh + s) % n_yh, 0, False)
    half, far = tok // 2, block(2)
    from_below = shift(far[:half], "yh", 1, n_yh)
    from_above = shift(far[half:], "yh", -1, n_yh)
    part, from_below, from_above = lax.optimization_barrier((part, from_below, from_above))
    zero = jnp.zeros((half, width), F32)
    up = block(1).astype(F32) + jnp.concatenate([from_below.astype(F32), zero], 0)
    down = block(-1).astype(F32) + jnp.concatenate([zero, from_above.astype(F32)], 0)
    came = [shift(up.astype(BF16), "yh", 1, n_yh), shift(down.astype(BF16), "yh", -1, n_yh)]

    part = lax.all_to_all(part, ("yl", "z"), 0, 0, tiled=True)
    part = jnp.sum(part.astype(F32), axis=0).astype(BF16)
    part = lax.all_to_all(jnp.broadcast_to(part, (n_yl * n_z,) + part.shape), ("yl", "z"), 0, 0, tiled=True)
    part = part.transpose(1, 0, 2).reshape(v_dev // n_x, width)
    part = lax.all_to_all(jnp.broadcast_to(part, (n_x,) + part.shape), "x", 0, 0, tiled=True)
    grad_hidden = (block(0).astype(F32) + sum(v.astype(F32) for v in came)).astype(BF16)
    grad_weight = part.reshape(v_dev, width)
    return token_loss, grad_hidden, grad_weight


def fine(mesh_devices, sizes):
    mesh = Mesh(mesh_devices.reshape(sizes), ("x", "yl", "z", "yh", "core"))

    def body(*args):
        return per_device(*args, n_x=sizes[0], n_yl=sizes[1], n_z=sizes[2], n_yh=sizes[3])

    tokens = ("x", "yl", "z", "yh", "core")
    return jax.shard_map(
        body,
        mesh=mesh,
        in_specs=(P(tokens, None), P(DP), P(DP), P(VOCAB, None)),
        out_specs=(P(tokens), P(tokens, None), P(VOCAB, None)),
        check_vma=False,
    )


def solution(mesh):
    return fine(mesh.devices, (4, 2, 8, 4, 2))
```

```python
import jax
import jax.numpy as jnp
from jax import lax
from jax.experimental import pallas as pl
from jax.experimental.pallas import tpu as pltpu
from jax.sharding import Mesh
from jax.sharding import PartitionSpec as P

F32, BF16 = jnp.float32, jnp.bfloat16
DP = ("x", "yl", "z")
VOCAB = ("yh", "core")


def shift(value, axis, step, size):
    return lax.ppermute(value, axis, [(i, (i + step) % size) for i in range(size)])


def swap(value):
    return shift(value, "core", 1, 2)


def by_core(value, core):
    return jnp.where(core == 0, value, value[::-1])


def gather_yh(hidden, small, yh, n_yh):
    half = hidden.shape[0] // 2
    low, high = hidden[:half], hidden[half:]
    up_low = shift(low, "yh", 1, n_yh)
    down_high = shift(high, "yh", -1, n_yh)
    up_low, down_high, low, high, small = lax.optimization_barrier((up_low, down_high, low, high, small))
    far_low = shift(up_low, "yh", 1, n_yh)
    far_high = shift(down_high, "yh", -1, n_yh)
    up_high = shift(high, "yh", 1, n_yh)
    down_low = shift(low, "yh", -1, n_yh)
    out = jnp.zeros((n_yh, 2, half, hidden.shape[1]), hidden.dtype)
    out = lax.dynamic_update_slice(out, hidden.reshape(1, 2, half, -1), (yh, 0, 0, 0))
    before, after, far = (yh - 1) % n_yh, (yh + 1) % n_yh, (yh + 2) % n_yh
    for piece, owner, part in (
        (up_low, before, 0),
        (down_high, after, 1),
        (far_low, far, 0),
        (far_high, far, 1),
        (up_high, before, 1),
        (down_low, after, 0),
    ):
        out = lax.dynamic_update_slice(out, piece[None, None], (owner, part, 0, 0))
    return out.reshape(n_yh * 2 * half, -1), small


def hits(where, labels, shape):
    return lax.broadcasted_iota(jnp.int32, shape, 0) + where[1] == labels


def local_stats(where, head, block, labels, logits):
    rows_t = (((1,), (1,)), ((), ()))
    value = lax.dot_general(head[...], block[...], rows_t, preferred_element_type=F32)
    logits[...] = value
    top = jnp.max(value, axis=0, keepdims=True)
    total = jnp.sum(jnp.exp(value - top), axis=0, keepdims=True)
    target = jnp.sum(jnp.where(hits(where, labels, value.shape), value, 0.0), axis=0, keepdims=True)
    return top, total, target


def own_kernel(where, head, block, labels, logits, stats):
    top, total, target = local_stats(where, head, block, labels[0:1], logits)
    stats[...] = jnp.zeros_like(stats)
    stats[0:1], stats[1:2], stats[2:3] = top, total, target


def other_kernel(where, head, block, labels, own_stats, logits, stats):
    ours = local_stats(where, head, block, labels[1:2], logits)
    first = where[0] == 0
    rows = [own_stats[i : i + 1] for i in range(3)]
    line = [jnp.where(first, rows[i], ours[i]) for i in range(3)] + [jnp.where(first, ours[i], rows[i]) for i in range(3)]
    blank = jnp.zeros_like(rows[0])
    tile = jnp.concatenate(line + [blank, blank], axis=0)
    for shard in range(stats.shape[0]):
        stats[shard] = tile


def score_kernel(where, stats, labels, weights, own_logits, other_logits, own, other, head, grad, away, score, loss, held):
    n_own = own_logits.shape[1]

    @pl.when(pl.program_id(0) == 0)
    def _():
        merged = []
        for c in range(2):
            top = jnp.max(stats[:, 3 * c], axis=0, keepdims=True)
            total = jnp.sum(stats[:, 3 * c + 1] * jnp.exp(stats[:, 3 * c] - top), axis=0, keepdims=True)
            log_total = top + jnp.log(total)
            merged.append((log_total, log_total - jnp.sum(stats[:, 3 * c + 2], axis=0, keepdims=True)))
        first = where[0] == 0
        loss[...] = jnp.where(first, merged[0][1], merged[1][1])
        for k, logits in enumerate((own_logits, other_logits)):
            log_total = jnp.where(first, merged[k][0], merged[1 - k][0])
            hit = hits(where, labels[k : k + 1], logits.shape).astype(F32)
            value = weights[k : k + 1] * (jnp.exp(logits[...] - log_total) - hit)
            held[:, k * n_own : (k + 1) * n_own] = value.astype(BF16)
        score[...] = held[:, :n_own]

    total = jnp.dot(held[:, :n_own], own[...], preferred_element_type=F32)
    total += jnp.dot(held[:, n_own:], other[...], preferred_element_type=F32)
    grad[...] = total.astype(BF16)
    rows_v = (((0,), (0,)), ((), ()))
    away[...] = lax.dot_general(held[:, n_own:], head[...], rows_v, preferred_element_type=F32).astype(BF16)


def per_device(hidden, targets, token_weight, head_weight, *, n_x, n_yl, n_z, n_yh):
    yh, core = lax.axis_index("yh"), lax.axis_index("core")
    tok, width = hidden.shape
    v_dev = head_weight.shape[0]
    n_own, n_shards = n_yh * tok, 2 * n_yh
    labels = by_core(targets.reshape(n_yh, 2, tok).transpose(1, 0, 2), core).reshape(2, n_own)
    weights = by_core(token_weight.reshape(n_yh, 2, tok).transpose(1, 0, 2), core).reshape(2, n_own)
    where = jnp.stack([core, (yh * 2 + core) * v_dev])

    own, (labels, weights, where) = gather_yh(hidden, (labels, weights, where), yh, n_yh)
    other = swap(own)

    smem, vmem = pl.BlockSpec(memory_space=pltpu.SMEM), pl.BlockSpec(memory_space=pltpu.VMEM)
    params = pltpu.CompilerParams(vmem_limit_bytes=32 << 20)
    cost = pl.CostEstimate(flops=2 * v_dev * n_own * width, bytes_accessed=2 * (v_dev + n_own) * width, transcendentals=v_dev * n_own)
    own_logits, stats = pl.pallas_call(
        own_kernel,
        out_shape=(jax.ShapeDtypeStruct((v_dev, n_own), F32), jax.ShapeDtypeStruct((8, n_own), F32)),
        in_specs=[smem, vmem, vmem, vmem],
        out_specs=(vmem, vmem),
        compiler_params=params,
        cost_estimate=cost,
    )(where, head_weight, own, labels)
    other_logits, stats = pl.pallas_call(
        other_kernel,
        out_shape=(jax.ShapeDtypeStruct((v_dev, n_own), F32), jax.ShapeDtypeStruct((n_shards, 8, n_own), F32)),
        in_specs=[smem, vmem, vmem, vmem, vmem],
        out_specs=(vmem, vmem),
        compiler_params=params,
        cost_estimate=cost,
    )(where, head_weight, other, labels, stats)
    stats = lax.all_to_all(stats, VOCAB, 0, 0, tiled=True)

    cols = min(1024, width)
    whole = lambda *shape: pl.BlockSpec(shape, lambda i: (0,) * len(shape))
    wide = lambda rows: pl.BlockSpec((rows, cols), lambda i: (0, i))
    partial, away, score, loss = pl.pallas_call(
        score_kernel,
        out_shape=(
            jax.ShapeDtypeStruct((v_dev, width), BF16),
            jax.ShapeDtypeStruct((n_own, width), BF16),
            jax.ShapeDtypeStruct((v_dev, n_own), BF16),
            jax.ShapeDtypeStruct((1, n_own), F32),
        ),
        grid=(width // cols,),
        in_specs=[
            smem,
            whole(n_shards, 8, n_own),
            whole(2, n_own),
            whole(2, n_own),
            whole(v_dev, n_own),
            whole(v_dev, n_own),
            wide(n_own),
            wide(n_own),
            wide(v_dev),
        ],
        out_specs=(wide(v_dev), wide(n_own), whole(v_dev, n_own), whole(1, n_own)),
        scratch_shapes=[pltpu.VMEM((v_dev, 2 * n_own), BF16)],
        compiler_params=params,
        cost_estimate=pl.CostEstimate(
            flops=6 * v_dev * n_own * width,
            bytes_accessed=2 * (2 * v_dev + 3 * n_own) * width,
            transcendentals=2 * v_dev * n_own,
        ),
    )(where, stats, labels, weights, own_logits, other_logits, own, other, head_weight)
    token_loss = lax.dynamic_slice_in_dim(loss[0], yh * tok, tok)

    part = partial.reshape(n_x, v_dev // n_x, width)
    part = lax.all_to_all(part, "x", 0, 0, tiled=True)
    part = jnp.sum(part.astype(F32), axis=0).astype(BF16)
    part = part.reshape(v_dev // n_x, n_yl * n_z, -1).transpose(1, 0, 2)

    rows_v = (((0,), (0,)), ((), ()))
    home = lax.dot_general(score, head_weight, rows_v, preferred_element_type=F32).astype(BF16)
    terms = (home.astype(F32) + swap(away).astype(F32)).astype(BF16).reshape(n_yh, tok, width)

    block = lambda s: lax.dynamic_index_in_dim(terms, (yh + s) % n_yh, 0, False)
    half, far = tok // 2, block(2)
    from_below = shift(far[:half], "yh", 1, n_yh)
    from_above = shift(far[half:], "yh", -1, n_yh)
    part, from_below, from_above = lax.optimization_barrier((part, from_below, from_above))
    zero = jnp.zeros((half, width), F32)
    up = block(1).astype(F32) + jnp.concatenate([from_below.astype(F32), zero], 0)
    down = block(-1).astype(F32) + jnp.concatenate([zero, from_above.astype(F32)], 0)
    came = [shift(up.astype(BF16), "yh", 1, n_yh), shift(down.astype(BF16), "yh", -1, n_yh)]

    part = lax.all_to_all(part, ("yl", "z"), 0, 0, tiled=True)
    part = jnp.sum(part.astype(F32), axis=0).astype(BF16)
    part = lax.all_to_all(jnp.broadcast_to(part, (n_yl * n_z,) + part.shape), ("yl", "z"), 0, 0, tiled=True)
    part = part.transpose(1, 0, 2).reshape(v_dev // n_x, width)
    part = lax.all_to_all(jnp.broadcast_to(part, (n_x,) + part.shape), "x", 0, 0, tiled=True)
    grad_weight = part.reshape(v_dev, width)

    grad_hidden = (block(0).astype(F32) + sum(v.astype(F32) for v in came)).astype(BF16)
    return token_loss, grad_hidden, grad_weight


def fine(mesh_devices, sizes):
    mesh = Mesh(mesh_devices.reshape(sizes), ("x", "yl", "z", "yh", "core"))

    def body(*args):
        return per_device(*args, n_x=sizes[0], n_yl=sizes[1], n_z=sizes[2], n_yh=sizes[3])

    tokens = ("x", "yl", "z", "yh", "core")
    return jax.shard_map(
        body,
        mesh=mesh,
        in_specs=(P(tokens, None), P(DP), P(DP), P(VOCAB, None)),
        out_specs=(P(tokens), P(tokens, None), P(VOCAB, None)),
        check_vma=False,
    )


def solution(mesh):
    return fine(mesh.devices, (4, 2, 8, 4, 2))
```

```python
import jax
import jax.numpy as jnp
from jax import lax
from jax.experimental import pallas as pl
from jax.experimental.pallas import tpu as pltpu
from jax.sharding import Mesh
from jax.sharding import PartitionSpec as P

F32, BF16 = jnp.float32, jnp.bfloat16
DP = ("x", "yl", "z")
VOCAB = ("yh", "core")


def shift(value, axis, step, size):
    return lax.ppermute(value, axis, [(i, (i + step) % size) for i in range(size)])


def swap(value):
    return shift(value, "core", 1, 2)


def by_core(value, core):
    return jnp.where(core == 0, value, value[::-1])


def gather_yh(hidden, small, yh, n_yh):
    half = hidden.shape[0] // 2
    low, high = hidden[:half], hidden[half:]
    up_low = shift(low, "yh", 1, n_yh)
    down_high = shift(high, "yh", -1, n_yh)
    up_high = shift(high, "yh", 1, n_yh)
    down_low = shift(low, "yh", -1, n_yh)
    up_low, down_high, small = lax.optimization_barrier((up_low, down_high, small))
    far_low = shift(up_low, "yh", 1, n_yh)
    far_high = shift(down_high, "yh", -1, n_yh)
    out = jnp.zeros((n_yh, 2, half, hidden.shape[1]), hidden.dtype)
    out = lax.dynamic_update_slice(out, hidden.reshape(1, 2, half, -1), (yh, 0, 0, 0))
    before, after, far = (yh - 1) % n_yh, (yh + 1) % n_yh, (yh + 2) % n_yh
    for piece, owner, part in (
        (up_low, before, 0),
        (down_high, after, 1),
        (far_low, far, 0),
        (far_high, far, 1),
        (up_high, before, 1),
        (down_low, after, 0),
    ):
        out = lax.dynamic_update_slice(out, piece[None, None], (owner, part, 0, 0))
    return out.reshape(n_yh * 2 * half, -1), small


def hits(where, labels, shape):
    return lax.broadcasted_iota(jnp.int32, shape, 0) + where[1] == labels


def local_stats(where, head, block, labels, logits):
    rows_t = (((1,), (1,)), ((), ()))
    value = lax.dot_general(head[...], block[...], rows_t, preferred_element_type=F32)
    logits[...] = value
    top = jnp.max(value, axis=0, keepdims=True)
    total = jnp.sum(jnp.exp(value - top), axis=0, keepdims=True)
    target = jnp.sum(jnp.where(hits(where, labels, value.shape), value, 0.0), axis=0, keepdims=True)
    return top, total, target


def own_kernel(where, head, block, labels, logits, stats):
    top, total, target = local_stats(where, head, block, labels[0:1], logits)
    stats[...] = jnp.zeros_like(stats)
    stats[0:1], stats[1:2], stats[2:3] = top, total, target


def other_kernel(where, head, block, labels, own_stats, logits, stats):
    ours = local_stats(where, head, block, labels[1:2], logits)
    first = where[0] == 0
    rows = [own_stats[i : i + 1] for i in range(3)]
    line = [jnp.where(first, rows[i], ours[i]) for i in range(3)] + [jnp.where(first, ours[i], rows[i]) for i in range(3)]
    blank = jnp.zeros_like(rows[0])
    tile = jnp.concatenate(line + [blank, blank], axis=0)
    for shard in range(stats.shape[0]):
        stats[shard] = tile


def score_kernel(where, stats, labels, weights, own_logits, other_logits, own, other, head, grad, away, score, loss, held):
    n_own = own_logits.shape[1]

    @pl.when(pl.program_id(0) == 0)
    def _():
        merged = []
        for c in range(2):
            top = jnp.max(stats[:, 3 * c], axis=0, keepdims=True)
            total = jnp.sum(stats[:, 3 * c + 1] * jnp.exp(stats[:, 3 * c] - top), axis=0, keepdims=True)
            log_total = top + jnp.log(total)
            merged.append((log_total, log_total - jnp.sum(stats[:, 3 * c + 2], axis=0, keepdims=True)))
        first = where[0] == 0
        loss[...] = jnp.where(first, merged[0][1], merged[1][1])
        for k, logits in enumerate((own_logits, other_logits)):
            log_total = jnp.where(first, merged[k][0], merged[1 - k][0])
            hit = hits(where, labels[k : k + 1], logits.shape).astype(F32)
            value = weights[k : k + 1] * (jnp.exp(logits[...] - log_total) - hit)
            held[:, k * n_own : (k + 1) * n_own] = value.astype(BF16)
        score[...] = held[:, :n_own]

    total = jnp.dot(held[:, :n_own], own[...], preferred_element_type=F32)
    total += jnp.dot(held[:, n_own:], other[...], preferred_element_type=F32)
    grad[...] = total.astype(BF16)
    rows_v = (((0,), (0,)), ((), ()))
    away[...] = lax.dot_general(held[:, n_own:], head[...], rows_v, preferred_element_type=F32).astype(BF16)


def lay_kernel(pieces, out):
    cols = pieces.shape[3]
    for i in range(pieces.shape[1]):
        out[:, i * cols : (i + 1) * cols] = pieces[0, i]


def per_device(hidden, targets, token_weight, head_weight, *, n_x, n_yl, n_z, n_yh):
    yh, core = lax.axis_index("yh"), lax.axis_index("core")
    tok, width = hidden.shape
    v_dev = head_weight.shape[0]
    n_own, n_shards = n_yh * tok, 2 * n_yh
    labels = by_core(targets.reshape(n_yh, 2, tok).transpose(1, 0, 2), core).reshape(2, n_own)
    weights = by_core(token_weight.reshape(n_yh, 2, tok).transpose(1, 0, 2), core).reshape(2, n_own)
    where = jnp.stack([core, (yh * 2 + core) * v_dev])

    own, (labels, weights, where) = gather_yh(hidden, (labels, weights, where), yh, n_yh)
    other = swap(own)

    smem, vmem = pl.BlockSpec(memory_space=pltpu.SMEM), pl.BlockSpec(memory_space=pltpu.VMEM)
    params = pltpu.CompilerParams(vmem_limit_bytes=32 << 20)
    cost = pl.CostEstimate(flops=2 * v_dev * n_own * width, bytes_accessed=2 * (v_dev + n_own) * width, transcendentals=v_dev * n_own)
    own_logits, stats = pl.pallas_call(
        own_kernel,
        out_shape=(jax.ShapeDtypeStruct((v_dev, n_own), F32), jax.ShapeDtypeStruct((8, n_own), F32)),
        in_specs=[smem, vmem, vmem, vmem],
        out_specs=(vmem, vmem),
        compiler_params=params,
        cost_estimate=cost,
    )(where, head_weight, own, labels)
    other_logits, stats = pl.pallas_call(
        other_kernel,
        out_shape=(jax.ShapeDtypeStruct((v_dev, n_own), F32), jax.ShapeDtypeStruct((n_shards, 8, n_own), F32)),
        in_specs=[smem, vmem, vmem, vmem, vmem],
        out_specs=(vmem, vmem),
        compiler_params=params,
        cost_estimate=cost,
    )(where, head_weight, other, labels, stats)
    stats = lax.all_to_all(stats, VOCAB, 0, 0, tiled=True)

    cols = min(1024, width)
    whole = lambda *shape: pl.BlockSpec(shape, lambda i: (0,) * len(shape))
    wide = lambda rows: pl.BlockSpec((rows, cols), lambda i: (0, i))
    partial, away, score, loss = pl.pallas_call(
        score_kernel,
        out_shape=(
            jax.ShapeDtypeStruct((v_dev, width), BF16),
            jax.ShapeDtypeStruct((n_own, width), BF16),
            jax.ShapeDtypeStruct((v_dev, n_own), BF16),
            jax.ShapeDtypeStruct((1, n_own), F32),
        ),
        grid=(width // cols,),
        in_specs=[
            smem,
            whole(n_shards, 8, n_own),
            whole(2, n_own),
            whole(2, n_own),
            whole(v_dev, n_own),
            whole(v_dev, n_own),
            wide(n_own),
            wide(n_own),
            wide(v_dev),
        ],
        out_specs=(wide(v_dev), wide(n_own), whole(v_dev, n_own), whole(1, n_own)),
        scratch_shapes=[pltpu.VMEM((v_dev, 2 * n_own), BF16)],
        compiler_params=params,
        cost_estimate=pl.CostEstimate(
            flops=6 * v_dev * n_own * width,
            bytes_accessed=2 * (2 * v_dev + 3 * n_own) * width,
            transcendentals=2 * v_dev * n_own,
        ),
    )(where, stats, labels, weights, own_logits, other_logits, own, other, head_weight)
    token_loss = lax.dynamic_slice_in_dim(loss[0], yh * tok, tok)

    part = partial.reshape(n_x, v_dev // n_x, width)
    part = lax.all_to_all(part, "x", 0, 0, tiled=True)

    rows_v = (((0,), (0,)), ((), ()))
    home = lax.dot_general(score, head_weight, rows_v, preferred_element_type=F32).astype(BF16)
    terms = (home.astype(F32) + swap(away).astype(F32)).astype(BF16)

    part, terms = lax.optimization_barrier((part, terms))
    part = jnp.sum(part.astype(F32), axis=0).astype(BF16)
    part = part.reshape(v_dev // n_x, n_yl * n_z, -1).transpose(1, 0, 2)
    grad_hidden = lax.psum_scatter(terms, "yh", scatter_dimension=0, tiled=True)

    part = lax.all_to_all(part, ("yl", "z"), 0, 0, tiled=True)
    part = jnp.sum(part.astype(F32), axis=0).astype(BF16)
    part = lax.all_to_all(jnp.broadcast_to(part, (n_yl * n_z,) + part.shape), ("yl", "z"), 0, 0, tiled=True)
    part = lax.all_to_all(jnp.broadcast_to(part, (n_x,) + part.shape), "x", 0, 0, tiled=True)
    grad_weight = pl.pallas_call(
        lay_kernel,
        out_shape=jax.ShapeDtypeStruct((v_dev, width), BF16),
        grid=(n_x,),
        in_specs=[pl.BlockSpec((1,) + part.shape[1:], lambda i: (i, 0, 0, 0))],
        out_specs=pl.BlockSpec((v_dev // n_x, width), lambda i: (i, 0)),
        compiler_params=params,
        cost_estimate=pl.CostEstimate(flops=0, bytes_accessed=4 * v_dev * width, transcendentals=0),
    )(part)
    return token_loss, grad_hidden, grad_weight


def fine(mesh_devices, sizes):
    mesh = Mesh(mesh_devices.reshape(sizes), ("x", "yl", "z", "yh", "core"))

    def body(*args):
        return per_device(*args, n_x=sizes[0], n_yl=sizes[1], n_z=sizes[2], n_yh=sizes[3])

    tokens = ("x", "yl", "z", "yh", "core")
    return jax.shard_map(
        body,
        mesh=mesh,
        in_specs=(P(tokens, None), P(DP), P(DP), P(VOCAB, None)),
        out_specs=(P(tokens), P(tokens, None), P(VOCAB, None)),
        check_vma=False,
    )


def solution(mesh):
    return fine(mesh.devices, (4, 2, 8, 4, 2))
```

```python
import jax
import jax.numpy as jnp
from jax import lax
from jax.experimental import pallas as pl
from jax.experimental.pallas import tpu as pltpu
from jax.sharding import Mesh
from jax.sharding import PartitionSpec as P

F32, BF16 = jnp.float32, jnp.bfloat16
DP = ("x", "yl", "z")
VOCAB = ("yh", "core")


def shift(value, axis, step, size):
    return lax.ppermute(value, axis, [(i, (i + step) % size) for i in range(size)])


def swap(value):
    return shift(value, "core", 1, 2)


def by_core(value, core):
    return jnp.where(core == 0, value, value[::-1])


def gather_yh(hidden, small, yh, n_yh):
    half = hidden.shape[0] // 2
    low, high = hidden[:half], hidden[half:]
    up_low = shift(low, "yh", 1, n_yh)
    down_high = shift(high, "yh", -1, n_yh)
    up_high = shift(high, "yh", 1, n_yh)
    down_low = shift(low, "yh", -1, n_yh)
    up_low, down_high, small = lax.optimization_barrier((up_low, down_high, small))
    far_low = shift(up_low, "yh", 1, n_yh)
    far_high = shift(down_high, "yh", -1, n_yh)
    out = jnp.zeros((n_yh, 2, half, hidden.shape[1]), hidden.dtype)
    out = lax.dynamic_update_slice(out, hidden.reshape(1, 2, half, -1), (yh, 0, 0, 0))
    before, after, far = (yh - 1) % n_yh, (yh + 1) % n_yh, (yh + 2) % n_yh
    for piece, owner, part in (
        (up_low, before, 0),
        (down_high, after, 1),
        (far_low, far, 0),
        (far_high, far, 1),
        (up_high, before, 1),
        (down_low, after, 0),
    ):
        out = lax.dynamic_update_slice(out, piece[None, None], (owner, part, 0, 0))
    return out.reshape(n_yh * 2 * half, -1), small


def hits(where, labels, shape):
    return lax.broadcasted_iota(jnp.int32, shape, 0) + where[1] == labels


def local_stats(where, head, block, labels, logits):
    rows_t = (((1,), (1,)), ((), ()))
    value = lax.dot_general(head[...], block[...], rows_t, preferred_element_type=F32)
    logits[...] = value
    top = jnp.max(value, axis=0, keepdims=True)
    total = jnp.sum(jnp.exp(value - top), axis=0, keepdims=True)
    target = jnp.sum(jnp.where(hits(where, labels, value.shape), value, 0.0), axis=0, keepdims=True)
    return top, total, target


def own_kernel(where, head, block, labels, logits, stats):
    top, total, target = local_stats(where, head, block, labels[0:1], logits)
    stats[...] = jnp.zeros_like(stats)
    stats[0:1], stats[1:2], stats[2:3] = top, total, target


def other_kernel(where, head, block, labels, own_stats, logits, stats):
    ours = local_stats(where, head, block, labels[1:2], logits)
    first = where[0] == 0
    rows = [own_stats[i : i + 1] for i in range(3)]
    line = [jnp.where(first, rows[i], ours[i]) for i in range(3)] + [jnp.where(first, ours[i], rows[i]) for i in range(3)]
    blank = jnp.zeros_like(rows[0])
    tile = jnp.concatenate(line + [blank, blank], axis=0)
    for shard in range(stats.shape[0]):
        stats[shard] = tile


def score_kernel(where, stats, labels, weights, own_logits, other_logits, own, other, head, grad, away, score, loss, held):
    n_own = own_logits.shape[1]

    @pl.when(pl.program_id(0) == 0)
    def _():
        merged = []
        for c in range(2):
            top = jnp.max(stats[:, 3 * c], axis=0, keepdims=True)
            total = jnp.sum(stats[:, 3 * c + 1] * jnp.exp(stats[:, 3 * c] - top), axis=0, keepdims=True)
            log_total = top + jnp.log(total)
            merged.append((log_total, log_total - jnp.sum(stats[:, 3 * c + 2], axis=0, keepdims=True)))
        first = where[0] == 0
        loss[...] = jnp.where(first, merged[0][1], merged[1][1])
        for k, logits in enumerate((own_logits, other_logits)):
            log_total = jnp.where(first, merged[k][0], merged[1 - k][0])
            hit = hits(where, labels[k : k + 1], logits.shape).astype(F32)
            value = weights[k : k + 1] * (jnp.exp(logits[...] - log_total) - hit)
            held[:, k * n_own : (k + 1) * n_own] = value.astype(BF16)
        score[...] = held[:, :n_own]

    total = jnp.dot(held[:, :n_own], own[...], preferred_element_type=F32)
    total += jnp.dot(held[:, n_own:], other[...], preferred_element_type=F32)
    grad[...] = total.astype(BF16)
    rows_v = (((0,), (0,)), ((), ()))
    away[...] = lax.dot_general(held[:, n_own:], head[...], rows_v, preferred_element_type=F32).astype(BF16)


def lay_kernel(pieces, out):
    cols = pieces.shape[3]
    for i in range(pieces.shape[1]):
        out[:, i * cols : (i + 1) * cols] = pieces[0, i]


def per_device(hidden, targets, token_weight, head_weight, *, n_x, n_yl, n_z, n_yh):
    yh, core = lax.axis_index("yh"), lax.axis_index("core")
    tok, width = hidden.shape
    v_dev = head_weight.shape[0]
    n_own, n_shards = n_yh * tok, 2 * n_yh
    labels = by_core(targets.reshape(n_yh, 2, tok).transpose(1, 0, 2), core).reshape(2, n_own)
    weights = by_core(token_weight.reshape(n_yh, 2, tok).transpose(1, 0, 2), core).reshape(2, n_own)
    where = jnp.stack([core, (yh * 2 + core) * v_dev])

    own, (labels, weights, where) = gather_yh(hidden, (labels, weights, where), yh, n_yh)
    other = swap(own)

    smem, vmem = pl.BlockSpec(memory_space=pltpu.SMEM), pl.BlockSpec(memory_space=pltpu.VMEM)
    params = pltpu.CompilerParams(vmem_limit_bytes=32 << 20)
    cost = pl.CostEstimate(flops=2 * v_dev * n_own * width, bytes_accessed=2 * (v_dev + n_own) * width, transcendentals=v_dev * n_own)
    own_logits, stats = pl.pallas_call(
        own_kernel,
        out_shape=(jax.ShapeDtypeStruct((v_dev, n_own), F32), jax.ShapeDtypeStruct((8, n_own), F32)),
        in_specs=[smem, vmem, vmem, vmem],
        out_specs=(vmem, vmem),
        compiler_params=params,
        cost_estimate=cost,
    )(where, head_weight, own, labels)
    other_logits, stats = pl.pallas_call(
        other_kernel,
        out_shape=(jax.ShapeDtypeStruct((v_dev, n_own), F32), jax.ShapeDtypeStruct((n_shards, 8, n_own), F32)),
        in_specs=[smem, vmem, vmem, vmem, vmem],
        out_specs=(vmem, vmem),
        compiler_params=params,
        cost_estimate=cost,
    )(where, head_weight, other, labels, stats)
    stats = lax.all_to_all(stats, VOCAB, 0, 0, tiled=True)

    cols = min(1024, width)
    whole = lambda *shape: pl.BlockSpec(shape, lambda i: (0,) * len(shape))
    wide = lambda rows: pl.BlockSpec((rows, cols), lambda i: (0, i))
    partial, away, score, loss = pl.pallas_call(
        score_kernel,
        out_shape=(
            jax.ShapeDtypeStruct((v_dev, width), BF16),
            jax.ShapeDtypeStruct((n_own, width), BF16),
            jax.ShapeDtypeStruct((v_dev, n_own), BF16),
            jax.ShapeDtypeStruct((1, n_own), F32),
        ),
        grid=(width // cols,),
        in_specs=[
            smem,
            whole(n_shards, 8, n_own),
            whole(2, n_own),
            whole(2, n_own),
            whole(v_dev, n_own),
            whole(v_dev, n_own),
            wide(n_own),
            wide(n_own),
            wide(v_dev),
        ],
        out_specs=(wide(v_dev), wide(n_own), whole(v_dev, n_own), whole(1, n_own)),
        scratch_shapes=[pltpu.VMEM((v_dev, 2 * n_own), BF16)],
        compiler_params=params,
        cost_estimate=pl.CostEstimate(
            flops=6 * v_dev * n_own * width,
            bytes_accessed=2 * (2 * v_dev + 3 * n_own) * width,
            transcendentals=2 * v_dev * n_own,
        ),
    )(where, stats, labels, weights, own_logits, other_logits, own, other, head_weight)
    token_loss = lax.dynamic_slice_in_dim(loss[0], yh * tok, tok)

    part = partial.reshape(n_x, v_dev // n_x, width)
    part = lax.all_to_all(part, "x", 0, 0, tiled=True)

    rows_v = (((0,), (0,)), ((), ()))
    home = lax.dot_general(score, head_weight, rows_v, preferred_element_type=F32).astype(BF16)
    terms = (home.astype(F32) + swap(away).astype(F32)).astype(BF16)

    part = jnp.sum(part.astype(F32), axis=0).astype(BF16)
    part = part.reshape(v_dev // n_x, n_yl * n_z, -1).transpose(1, 0, 2)

    terms = terms.reshape(n_yh, tok, width)
    block = lambda s: lax.dynamic_index_in_dim(terms, (yh + s) % n_yh, 0, False)
    half, far = tok // 2, block(2)
    from_below = shift(far[:half], "yh", 1, n_yh)
    from_above = shift(far[half:], "yh", -1, n_yh)
    part, from_below, from_above = lax.optimization_barrier((part, from_below, from_above))
    zero = jnp.zeros((half, width), F32)
    up = block(1).astype(F32) + jnp.concatenate([from_below.astype(F32), zero], 0)
    down = block(-1).astype(F32) + jnp.concatenate([zero, from_above.astype(F32)], 0)
    came = [shift(up.astype(BF16), "yh", 1, n_yh), shift(down.astype(BF16), "yh", -1, n_yh)]

    part = lax.all_to_all(part, ("yl", "z"), 0, 0, tiled=True)
    part = jnp.sum(part.astype(F32), axis=0).astype(BF16)
    part = lax.all_to_all(jnp.broadcast_to(part, (n_yl * n_z,) + part.shape), ("yl", "z"), 0, 0, tiled=True)
    part = lax.all_to_all(jnp.broadcast_to(part, (n_x,) + part.shape), "x", 0, 0, tiled=True)
    grad_weight = pl.pallas_call(
        lay_kernel,
        out_shape=jax.ShapeDtypeStruct((v_dev, width), BF16),
        grid=(n_x,),
        in_specs=[pl.BlockSpec((1,) + part.shape[1:], lambda i: (i, 0, 0, 0))],
        out_specs=pl.BlockSpec((v_dev // n_x, width), lambda i: (i, 0)),
        compiler_params=params,
        cost_estimate=pl.CostEstimate(flops=0, bytes_accessed=4 * v_dev * width, transcendentals=0),
    )(part)
    grad_hidden = (block(0).astype(F32) + sum(v.astype(F32) for v in came)).astype(BF16)
    return token_loss, grad_hidden, grad_weight


def fine(mesh_devices, sizes):
    mesh = Mesh(mesh_devices.reshape(sizes), ("x", "yl", "z", "yh", "core"))

    def body(*args):
        return per_device(*args, n_x=sizes[0], n_yl=sizes[1], n_z=sizes[2], n_yh=sizes[3])

    tokens = ("x", "yl", "z", "yh", "core")
    return jax.shard_map(
        body,
        mesh=mesh,
        in_specs=(P(tokens, None), P(DP), P(DP), P(VOCAB, None)),
        out_specs=(P(tokens), P(tokens, None), P(VOCAB, None)),
        check_vma=False,
    )


def solution(mesh):
    return fine(mesh.devices, (4, 2, 8, 4, 2))
```

```python
import jax
import jax.numpy as jnp
from jax import lax
from jax.experimental import pallas as pl
from jax.experimental.pallas import tpu as pltpu
from jax.sharding import Mesh
from jax.sharding import PartitionSpec as P

F32, BF16 = jnp.float32, jnp.bfloat16
DP = ("x", "yl", "z")
VOCAB = ("yh", "core")


def shift(value, axis, step, size):
    return lax.ppermute(value, axis, [(i, (i + step) % size) for i in range(size)])


def swap(value):
    return shift(value, "core", 1, 2)


def hits(where, labels, shape):
    return lax.broadcasted_iota(jnp.int32, shape, 0) + where[1] == labels


def block_stats(where, head, pieces, labels, logits):
    rows_t = (((1,), (1,)), ((), ()))
    block = jnp.concatenate([piece[...] for piece in pieces], axis=0)
    value = lax.dot_general(head[...], block, rows_t, preferred_element_type=F32)
    logits[...] = value
    top = jnp.max(value, axis=0, keepdims=True)
    total = jnp.sum(jnp.exp(value - top), axis=0, keepdims=True)
    target = jnp.sum(jnp.where(hits(where, labels, value.shape), value, 0.0), axis=0, keepdims=True)
    blank = jnp.zeros_like(top)
    tile = jnp.concatenate([top, total, target] + [blank] * 5, axis=0)
    return jnp.where(where[0] == 0, tile, pltpu.roll(tile, tile.shape[1] // 2, 1))


def near_kernel(where, head, labels, *refs):
    pieces, logits, stats = refs[:6], refs[6:9], refs[9]
    n = logits[0].shape[1]
    for m in range(3):
        lanes = slice(m * n, (m + 1) * n)
        stats[:, lanes] = block_stats(where, head, pieces[2 * m : 2 * m + 2], labels[:, lanes], logits[m])


def far_kernel(where, head, labels, near, *refs):
    pieces, logits, stats = refs[:4], refs[4], refs[5]
    n = logits.shape[1]
    tiles = [near[:, m * n : (m + 1) * n] for m in range(3)]
    tiles.append(block_stats(where, head, pieces, labels[:, 3 * n :], logits))
    for m, tile in enumerate(tiles):
        at = pl.multiple_of(where[2 + m] * 8, 8)
        for shard in range(stats.shape[0]):
            stats[shard, pl.ds(at, 8), :] = tile


def score_kernel(where, stats, labels, weights, *refs):
    all_logits, pieces, head = refs[:4], refs[4:14], refs[14]
    grad, away, score, loss, held, turned = refs[15:]
    n = all_logits[0].shape[1]
    half = n // 2

    @pl.when(pl.program_id(0) == 0)
    def _():
        for m, logits in enumerate(all_logits):
            lanes = slice(m * n, (m + 1) * n)
            part = stats[:, pl.ds(pl.multiple_of(where[2 + m] * 8, 8), 8), :]
            tops = part[:, 0, :]
            top = jnp.max(tops, axis=0, keepdims=True)
            total = jnp.sum(part[:, 1, :] * jnp.exp(tops - top), axis=0, keepdims=True)
            log_total = top + jnp.log(total)
            lost = log_total - jnp.sum(part[:, 2, :], axis=0, keepdims=True)
            both = jnp.concatenate([log_total, lost] + [jnp.zeros_like(top)] * 6, axis=0)
            both = jnp.where(where[0] == 0, both, pltpu.roll(both, half, 1))
            if m == 0:
                loss[...] = both[1:2]
            hit = hits(where, labels[:, lanes], logits.shape).astype(F32)
            value = weights[:, lanes] * (jnp.exp(logits[...] - both[0:1]) - hit)
            held[:, lanes] = value.astype(BF16)
            value = value.T.astype(BF16)
            score[m * half : (m + 1) * half] = value[:half]
            turned[m * half : (m + 1) * half] = value[half:]

    block = jnp.concatenate([piece[...] for piece in pieces], axis=0)
    grad[...] = jnp.dot(held[...], block, preferred_element_type=F32).astype(BF16)
    away[...] = jnp.dot(turned[...], head[...], preferred_element_type=F32).astype(BF16)


def lay_kernel(pieces, out):
    cols = pieces.shape[3]
    for i in range(pieces.shape[1]):
        out[:, i * cols : (i + 1) * cols] = pieces[0, i]


def per_device(hidden, targets, token_weight, head_weight, *, n_x, n_yl, n_z, n_yh):
    yh, core = lax.axis_index("yh"), lax.axis_index("core")
    tok, width = hidden.shape
    v_dev = head_weight.shape[0]
    half, both, n_own, n_shards = tok // 2, 2 * tok, n_yh * tok, 2 * n_yh

    def local_order(value):
        value = value.reshape(n_yh, 2, tok)
        value = lax.dynamic_slice_in_dim(jnp.concatenate([value, value], 0), yh, n_yh, 0)
        value = jnp.where(core == 0, value, value[:, ::-1])
        return jnp.concatenate([value[0], value[3], value[1], value[2]], 0).reshape(1, -1)

    labels, weights = local_order(targets), local_order(token_weight)
    where = jnp.stack([core, (yh * 2 + core) * v_dev] + [(yh + d) % n_yh for d in (0, n_yh - 1, 1, 2)])

    before = shift(hidden, "yh", 1, n_yh)
    after = shift(hidden, "yh", -1, n_yh)
    own_other = swap(hidden)
    before, labels, weights, where = lax.optimization_barrier((before, labels, weights, where))
    low, high, before, after = lax.optimization_barrier((before[:half], after[half:], before, after))
    far_low = shift(low, "yh", 1, n_yh)
    far_high = shift(high, "yh", -1, n_yh)
    near = (hidden, own_other, before, swap(before), after, swap(after))

    smem, vmem = pl.BlockSpec(memory_space=pltpu.SMEM), pl.BlockSpec(memory_space=pltpu.VMEM)
    params = pltpu.CompilerParams(vmem_limit_bytes=32 << 20)
    block_logits = jax.ShapeDtypeStruct((v_dev, both), F32)

    def cost(blocks):
        return pl.CostEstimate(
            flops=2 * v_dev * blocks * both * width,
            bytes_accessed=2 * (v_dev + blocks * both) * width,
            transcendentals=v_dev * blocks * both,
        )

    *near_logits, stats = pl.pallas_call(
        near_kernel,
        out_shape=(block_logits,) * 3 + (jax.ShapeDtypeStruct((8, 3 * both), F32),),
        in_specs=[smem] + [vmem] * 8,
        out_specs=(vmem,) * 4,
        compiler_params=params,
        cost_estimate=cost(3),
    )(where, head_weight, labels, *near)
    far_low, far_high, *near_logits, stats = lax.optimization_barrier((far_low, far_high, *near_logits, stats))
    far = (far_low, far_high, swap(far_low), swap(far_high))
    far_logits, stats = pl.pallas_call(
        far_kernel,
        out_shape=(block_logits, jax.ShapeDtypeStruct((n_shards, 8 * n_yh, both), F32)),
        in_specs=[smem] + [vmem] * 7,
        out_specs=(vmem,) * 2,
        compiler_params=params,
        cost_estimate=cost(1),
    )(where, head_weight, labels, stats, *far)
    stats = lax.all_to_all(stats, VOCAB, 0, 0, tiled=True)

    cols = min(1024, width)
    whole = lambda *shape: pl.BlockSpec(shape, lambda i: (0,) * len(shape))
    wide = lambda rows: pl.BlockSpec((rows, cols), lambda i: (0, i))
    partial, away, score, loss = pl.pallas_call(
        score_kernel,
        out_shape=(
            jax.ShapeDtypeStruct((v_dev, width), BF16),
            jax.ShapeDtypeStruct((n_own, width), BF16),
            jax.ShapeDtypeStruct((n_own, v_dev), BF16),
            jax.ShapeDtypeStruct((1, both), F32),
        ),
        grid=(width // cols,),
        in_specs=[smem, whole(*stats.shape), whole(1, 2 * n_own), whole(1, 2 * n_own)]
        + [whole(v_dev, both)] * 4
        + [wide(tok)] * 6
        + [wide(half)] * 4
        + [wide(v_dev)],
        out_specs=(wide(v_dev), wide(n_own), whole(n_own, v_dev), whole(1, both)),
        scratch_shapes=[pltpu.VMEM((v_dev, 2 * n_own), BF16), pltpu.VMEM((n_own, v_dev), BF16)],
        compiler_params=params,
        cost_estimate=pl.CostEstimate(
            flops=6 * v_dev * n_own * width,
            bytes_accessed=2 * (2 * v_dev + 3 * n_own) * width,
            transcendentals=2 * v_dev * n_own,
        ),
    )(where, stats, labels, weights, *near_logits, far_logits, *near, *far, head_weight)
    token_loss = loss[0, :tok]

    part = partial.reshape(n_x, v_dev // n_x, width)
    part = lax.all_to_all(part, "x", 0, 0, tiled=True)

    home = jnp.dot(score, head_weight, preferred_element_type=F32).astype(BF16)
    terms = (home.astype(F32) + swap(away).astype(F32)).astype(BF16)
    part = jnp.sum(part.astype(F32), axis=0).astype(BF16)
    part = part.reshape(v_dev // n_x, n_yl * n_z, -1).transpose(1, 0, 2)

    mine, up, down, far = (terms[m * tok : (m + 1) * tok] for m in (0, 2, 1, 3))
    from_below = shift(far[:half], "yh", 1, n_yh)
    from_above = shift(far[half:], "yh", -1, n_yh)
    part, from_below, from_above = lax.optimization_barrier((part, from_below, from_above))
    zero = jnp.zeros((half, width), F32)
    up = up.astype(F32) + jnp.concatenate([from_below.astype(F32), zero], 0)
    down = down.astype(F32) + jnp.concatenate([zero, from_above.astype(F32)], 0)
    came = [shift(up.astype(BF16), "yh", 1, n_yh), shift(down.astype(BF16), "yh", -1, n_yh)]

    part = lax.all_to_all(part, ("yl", "z"), 0, 0, tiled=True)
    part = jnp.sum(part.astype(F32), axis=0).astype(BF16)
    part = lax.all_to_all(jnp.broadcast_to(part, (n_yl * n_z,) + part.shape), ("yl", "z"), 0, 0, tiled=True)
    part = lax.all_to_all(jnp.broadcast_to(part, (n_x,) + part.shape), "x", 0, 0, tiled=True)
    grad_weight = pl.pallas_call(
        lay_kernel,
        out_shape=jax.ShapeDtypeStruct((v_dev, width), BF16),
        grid=(n_x,),
        in_specs=[pl.BlockSpec((1,) + part.shape[1:], lambda i: (i, 0, 0, 0))],
        out_specs=pl.BlockSpec((v_dev // n_x, width), lambda i: (i, 0)),
        compiler_params=params,
        cost_estimate=pl.CostEstimate(flops=0, bytes_accessed=4 * v_dev * width, transcendentals=0),
    )(part)
    grad_hidden = (mine.astype(F32) + sum(v.astype(F32) for v in came)).astype(BF16)
    return token_loss, grad_hidden, grad_weight


def fine(mesh_devices, sizes):
    mesh = Mesh(mesh_devices.reshape(sizes), ("x", "yl", "z", "yh", "core"))

    def body(*args):
        return per_device(*args, n_x=sizes[0], n_yl=sizes[1], n_z=sizes[2], n_yh=sizes[3])

    tokens = ("x", "yl", "z", "yh", "core")
    return jax.shard_map(
        body,
        mesh=mesh,
        in_specs=(P(tokens, None), P(DP), P(DP), P(VOCAB, None)),
        out_specs=(P(tokens), P(tokens, None), P(VOCAB, None)),
        check_vma=False,
    )


def solution(mesh):
    return fine(mesh.devices, (4, 2, 8, 4, 2))
```

```python
import jax
import jax.numpy as jnp
from jax import lax
from jax.experimental import pallas as pl
from jax.experimental.pallas import tpu as pltpu
from jax.sharding import Mesh
from jax.sharding import PartitionSpec as P

F32, BF16 = jnp.float32, jnp.bfloat16
DP = ("x", "yl", "z")
VOCAB = ("yh", "core")


def shift(value, axis, step, size):
    return lax.ppermute(value, axis, [(i, (i + step) % size) for i in range(size)])


def swap(value):
    return shift(value, "core", 1, 2)


def hits(where, labels, shape):
    return lax.broadcasted_iota(jnp.int32, shape, 0) + where[1] == labels


def block_stats(where, head, pieces, labels, logits):
    rows_t = (((1,), (1,)), ((), ()))
    block = jnp.concatenate([piece[...] for piece in pieces], axis=0)
    value = lax.dot_general(head[...], block, rows_t, preferred_element_type=F32)
    logits[...] = value
    top = jnp.max(value, axis=0, keepdims=True)
    total = jnp.sum(jnp.exp(value - top), axis=0, keepdims=True)
    target = jnp.sum(jnp.where(hits(where, labels, value.shape), value, 0.0), axis=0, keepdims=True)
    blank = jnp.zeros_like(top)
    tile = jnp.concatenate([top, total, target] + [blank] * 5, axis=0)
    return jnp.where(where[0] == 0, tile, pltpu.roll(tile, tile.shape[1] // 2, 1))


def near_kernel(where, head, labels, *refs):
    pieces, logits, stats = refs[:6], refs[6:9], refs[9]
    n = logits[0].shape[1]
    for m in range(3):
        lanes = slice(m * n, (m + 1) * n)
        stats[:, lanes] = block_stats(where, head, pieces[2 * m : 2 * m + 2], labels[:, lanes], logits[m])


def far_kernel(where, head, labels, near, *refs):
    pieces, logits, stats = refs[:4], refs[4], refs[5]
    n = logits.shape[1]
    tiles = [near[:, m * n : (m + 1) * n] for m in range(3)]
    tiles.append(block_stats(where, head, pieces, labels[:, 3 * n :], logits))
    for m, tile in enumerate(tiles):
        at = pl.multiple_of(where[2 + m] * 8, 8)
        for shard in range(stats.shape[0]):
            stats[shard, pl.ds(at, 8), :] = tile


def score_kernel(where, stats, labels, weights, *refs):
    all_logits, pieces, head = refs[:4], refs[4:14], refs[14]
    grad, away, score, loss, held, turned = refs[15:]
    n = all_logits[0].shape[1]
    half = n // 2

    @pl.when(pl.program_id(0) == 0)
    def _():
        for m, logits in enumerate(all_logits):
            lanes = slice(m * n, (m + 1) * n)
            part = stats[:, pl.ds(pl.multiple_of(where[2 + m] * 8, 8), 8), :]
            tops = part[:, 0, :]
            top = jnp.max(tops, axis=0, keepdims=True)
            total = jnp.sum(part[:, 1, :] * jnp.exp(tops - top), axis=0, keepdims=True)
            log_total = top + jnp.log(total)
            lost = log_total - jnp.sum(part[:, 2, :], axis=0, keepdims=True)
            both = jnp.concatenate([log_total, lost] + [jnp.zeros_like(top)] * 6, axis=0)
            both = jnp.where(where[0] == 0, both, pltpu.roll(both, half, 1))
            if m == 0:
                loss[...] = both[1:2]
            hit = hits(where, labels[:, lanes], logits.shape).astype(F32)
            value = weights[:, lanes] * (jnp.exp(logits[...] - both[0:1]) - hit)
            held[:, lanes] = value.astype(BF16)
            value = value.T.astype(BF16)
            score[m * half : (m + 1) * half] = value[:half]
            turned[m * half : (m + 1) * half] = value[half:]

    block = jnp.concatenate([piece[...] for piece in pieces], axis=0)
    grad[...] = jnp.dot(held[...], block, preferred_element_type=F32).astype(BF16)
    away[...] = jnp.dot(turned[...], head[...], preferred_element_type=F32).astype(BF16)


def sum_kernel(parts, out):
    cols = out.shape[2]
    for i in range(out.shape[0]):
        part = parts[:, :, i * cols : (i + 1) * cols].astype(F32)
        out[i] = jnp.sum(part, axis=0).astype(BF16)


def lay_kernel(where, own, before, after, far_low, far_high, out):
    n, rows, cols = own.shape
    for at, pieces in ((6, (own,)), (7, (before,)), (8, (after,)), (9, (far_low, far_high))):
        row = pl.ds(pl.multiple_of(where[at] * rows, rows), rows)
        pieces = [(piece, i) for piece in pieces for i in range(piece.shape[0])]
        for j, (piece, i) in enumerate(pieces):
            out[row, j * cols : (j + 1) * cols] = piece[i]


def per_device(hidden, targets, token_weight, head_weight, *, n_x, n_yl, n_z, n_yh):
    yh, core = lax.axis_index("yh"), lax.axis_index("core")
    tok, width = hidden.shape
    v_dev = head_weight.shape[0]
    half, both, n_own, n_shards = tok // 2, 2 * tok, n_yh * tok, 2 * n_yh

    def local_order(value):
        value = value.reshape(n_yh, 2, tok)
        value = lax.dynamic_slice_in_dim(jnp.concatenate([value, value], 0), yh, n_yh, 0)
        value = jnp.where(core == 0, value, value[:, ::-1])
        return jnp.concatenate([value[0], value[3], value[1], value[2]], 0).reshape(1, -1)

    labels, weights = local_order(targets), local_order(token_weight)
    where = [core, (yh * 2 + core) * v_dev] + [(yh + d) % n_yh for d in (0, n_yh - 1, 1, 2)]
    where = jnp.stack(where + [(lax.axis_index("x") + d) % n_x for d in (0, n_x - 1, 1, 2)])

    before = shift(hidden, "yh", 1, n_yh)
    after = shift(hidden, "yh", -1, n_yh)
    own_other = swap(hidden)
    before, labels, weights, where = lax.optimization_barrier((before, labels, weights, where))
    low, high, before, after = lax.optimization_barrier((before[:half], after[half:], before, after))
    far_low = shift(low, "yh", 1, n_yh)
    far_high = shift(high, "yh", -1, n_yh)
    near = (hidden, own_other, before, swap(before), after, swap(after))

    smem, vmem = pl.BlockSpec(memory_space=pltpu.SMEM), pl.BlockSpec(memory_space=pltpu.VMEM)
    params = pltpu.CompilerParams(vmem_limit_bytes=32 << 20)
    block_logits = jax.ShapeDtypeStruct((v_dev, both), F32)

    def cost(blocks):
        return pl.CostEstimate(
            flops=2 * v_dev * blocks * both * width,
            bytes_accessed=2 * (v_dev + blocks * both) * width,
            transcendentals=v_dev * blocks * both,
        )

    *near_logits, stats = pl.pallas_call(
        near_kernel,
        out_shape=(block_logits,) * 3 + (jax.ShapeDtypeStruct((8, 3 * both), F32),),
        in_specs=[smem] + [vmem] * 8,
        out_specs=(vmem,) * 4,
        compiler_params=params,
        cost_estimate=cost(3),
    )(where, head_weight, labels, *near)
    far_low, far_high, *near_logits, stats = lax.optimization_barrier((far_low, far_high, *near_logits, stats))
    far = (far_low, far_high, swap(far_low), swap(far_high))
    far_logits, stats = pl.pallas_call(
        far_kernel,
        out_shape=(block_logits, jax.ShapeDtypeStruct((n_shards, 8 * n_yh, both), F32)),
        in_specs=[smem] + [vmem] * 7,
        out_specs=(vmem,) * 2,
        compiler_params=params,
        cost_estimate=cost(1),
    )(where, head_weight, labels, stats, *far)
    stats = lax.all_to_all(stats, VOCAB, 0, 0, tiled=True)

    cols = min(1024, width)
    whole = lambda *shape: pl.BlockSpec(shape, lambda i: (0,) * len(shape))
    wide = lambda rows: pl.BlockSpec((rows, cols), lambda i: (0, i))
    partial, away, score, loss = pl.pallas_call(
        score_kernel,
        out_shape=(
            jax.ShapeDtypeStruct((v_dev, width), BF16),
            jax.ShapeDtypeStruct((n_own, width), BF16),
            jax.ShapeDtypeStruct((n_own, v_dev), BF16),
            jax.ShapeDtypeStruct((1, both), F32),
        ),
        grid=(width // cols,),
        in_specs=[smem, whole(*stats.shape), whole(1, 2 * n_own), whole(1, 2 * n_own)]
        + [whole(v_dev, both)] * 4
        + [wide(tok)] * 6
        + [wide(half)] * 4
        + [wide(v_dev)],
        out_specs=(wide(v_dev), wide(n_own), whole(n_own, v_dev), whole(1, both)),
        scratch_shapes=[pltpu.VMEM((v_dev, 2 * n_own), BF16), pltpu.VMEM((n_own, v_dev), BF16)],
        compiler_params=params,
        cost_estimate=pl.CostEstimate(
            flops=6 * v_dev * n_own * width,
            bytes_accessed=2 * (2 * v_dev + 3 * n_own) * width,
            transcendentals=2 * v_dev * n_own,
        ),
    )(where, stats, labels, weights, *near_logits, far_logits, *near, *far, head_weight)
    token_loss = loss[0, :tok]

    part = partial.reshape(n_x, v_dev // n_x, width)
    part = lax.all_to_all(part, "x", 0, 0, tiled=True)

    home = jnp.dot(score, head_weight, preferred_element_type=F32).astype(BF16)
    terms = (home.astype(F32) + swap(away).astype(F32)).astype(BF16)
    n_rest, rows = n_yl * n_z, v_dev // n_x
    step = min(4, n_rest)
    part = pl.pallas_call(
        sum_kernel,
        out_shape=jax.ShapeDtypeStruct((n_rest, rows, width // n_rest), BF16),
        grid=(n_rest // step,),
        in_specs=[pl.BlockSpec((n_x, rows, step * width // n_rest), lambda i: (0, 0, i))],
        out_specs=pl.BlockSpec((step, rows, width // n_rest), lambda i: (i, 0, 0)),
        compiler_params=params,
        cost_estimate=pl.CostEstimate(flops=v_dev * width, bytes_accessed=3 * v_dev * width, transcendentals=0),
    )(part)

    mine, up, down, far = (terms[m * tok : (m + 1) * tok] for m in (0, 2, 1, 3))
    from_below = shift(far[:half], "yh", 1, n_yh)
    from_above = shift(far[half:], "yh", -1, n_yh)
    part, from_below, from_above = lax.optimization_barrier((part, from_below, from_above))
    zero = jnp.zeros((half, width), F32)
    up = up.astype(F32) + jnp.concatenate([from_below.astype(F32), zero], 0)
    down = down.astype(F32) + jnp.concatenate([zero, from_above.astype(F32)], 0)
    came = [shift(up.astype(BF16), "yh", 1, n_yh), shift(down.astype(BF16), "yh", -1, n_yh)]

    part = lax.all_to_all(part, ("yl", "z"), 0, 0, tiled=True)
    part = jnp.sum(part.astype(F32), axis=0).astype(BF16)
    part = lax.all_to_all(jnp.broadcast_to(part, (n_yl * n_z,) + part.shape), ("yl", "z"), 0, 0, tiled=True)
    x_before = shift(part, "x", 1, n_x)
    x_after = shift(part, "x", -1, n_x)
    x_low = shift(x_before[: n_rest // 2], "x", 1, n_x)
    x_high = shift(x_after[n_rest // 2 :], "x", -1, n_x)
    grad_weight = pl.pallas_call(
        lay_kernel,
        out_shape=jax.ShapeDtypeStruct((v_dev, width), BF16),
        in_specs=[smem] + [vmem] * 5,
        out_specs=vmem,
        compiler_params=params,
        cost_estimate=pl.CostEstimate(flops=0, bytes_accessed=4 * v_dev * width, transcendentals=0),
    )(where, part, x_before, x_after, x_low, x_high)
    grad_hidden = (mine.astype(F32) + sum(v.astype(F32) for v in came)).astype(BF16)
    return token_loss, grad_hidden, grad_weight


def fine(mesh_devices, sizes):
    mesh = Mesh(mesh_devices.reshape(sizes), ("x", "yl", "z", "yh", "core"))

    def body(*args):
        return per_device(*args, n_x=sizes[0], n_yl=sizes[1], n_z=sizes[2], n_yh=sizes[3])

    tokens = ("x", "yl", "z", "yh", "core")
    return jax.shard_map(
        body,
        mesh=mesh,
        in_specs=(P(tokens, None), P(DP), P(DP), P(VOCAB, None)),
        out_specs=(P(tokens), P(tokens, None), P(VOCAB, None)),
        check_vma=False,
    )


def solution(mesh):
    return fine(mesh.devices, (4, 2, 8, 4, 2))
```

```python
import jax
import jax.numpy as jnp
from jax import lax
from jax.experimental import pallas as pl
from jax.experimental.pallas import tpu as pltpu
from jax.sharding import Mesh
from jax.sharding import PartitionSpec as P

F32, BF16 = jnp.float32, jnp.bfloat16
DP = ("x", "yl", "z")
VOCAB = ("yh", "core")


def shift(value, axis, step, size):
    return lax.ppermute(value, axis, [(i, (i + step) % size) for i in range(size)])


def swap(value):
    return shift(value, "core", 1, 2)


def hits(where, labels, shape):
    return lax.broadcasted_iota(jnp.int32, shape, 0) + where[1] == labels


def block_stats(where, head, pieces, labels, logits):
    rows_t = (((1,), (1,)), ((), ()))
    block = jnp.concatenate([piece[...] for piece in pieces], axis=0)
    value = lax.dot_general(head[...], block, rows_t, preferred_element_type=F32)
    logits[...] = value
    top = jnp.max(value, axis=0, keepdims=True)
    total = jnp.sum(jnp.exp(value - top), axis=0, keepdims=True)
    target = jnp.sum(jnp.where(hits(where, labels, value.shape), value, 0.0), axis=0, keepdims=True)
    blank = jnp.zeros_like(top)
    tile = jnp.concatenate([top, total, target] + [blank] * 5, axis=0)
    return jnp.where(where[0] == 0, tile, pltpu.roll(tile, tile.shape[1] // 2, 1))


def stage_kernel(head, own, head_out, own_out):
    head_out[...] = head[...]
    own_out[...] = own[...]


def logits_kernel(where, head, labels, *refs):
    pieces, logits, stats = refs[:10], refs[10:14], refs[14]
    n = logits[0].shape[1]
    for m, chosen in enumerate((pieces[:2], pieces[2:4], pieces[4:6], pieces[6:])):
        tile = block_stats(where, head, chosen, labels[:, m * n : (m + 1) * n], logits[m])
        at = pl.multiple_of(where[2 + m] * 8, 8)
        for shard in range(stats.shape[0]):
            stats[shard, pl.ds(at, 8), :] = tile


def score_kernel(where, stats, labels, weights, *refs):
    all_logits, pieces, head = refs[:4], refs[4:14], refs[14]
    grad, away, score, loss, held, turned = refs[15:]
    n = all_logits[0].shape[1]
    half = n // 2

    @pl.when(pl.program_id(0) == 0)
    def _():
        for m, logits in enumerate(all_logits):
            lanes = slice(m * n, (m + 1) * n)
            part = stats[:, pl.ds(pl.multiple_of(where[2 + m] * 8, 8), 8), :]
            tops = part[:, 0, :]
            top = jnp.max(tops, axis=0, keepdims=True)
            total = jnp.sum(part[:, 1, :] * jnp.exp(tops - top), axis=0, keepdims=True)
            log_total = top + jnp.log(total)
            lost = log_total - jnp.sum(part[:, 2, :], axis=0, keepdims=True)
            both = jnp.concatenate([log_total, lost] + [jnp.zeros_like(top)] * 6, axis=0)
            both = jnp.where(where[0] == 0, both, pltpu.roll(both, half, 1))
            if m == 0:
                loss[...] = both[1:2]
            hit = hits(where, labels[:, lanes], logits.shape).astype(F32)
            value = weights[:, lanes] * (jnp.exp(logits[...] - both[0:1]) - hit)
            held[:, lanes] = value.astype(BF16)
            value = value.T.astype(BF16)
            score[m * half : (m + 1) * half] = value[:half]
            turned[m * half : (m + 1) * half] = value[half:]

    block = jnp.concatenate([piece[...] for piece in pieces], axis=0)
    grad[...] = jnp.dot(held[...], block, preferred_element_type=F32).astype(BF16)
    away[...] = jnp.dot(turned[...], head[...], preferred_element_type=F32).astype(BF16)


def sum_kernel(parts, out):
    cols = out.shape[2]
    for i in range(out.shape[0]):
        part = parts[:, :, i * cols : (i + 1) * cols].astype(F32)
        out[i] = jnp.sum(part, axis=0).astype(BF16)


def lay_kernel(where, own, before, after, far_low, far_high, out):
    n, rows, cols = own.shape
    for at, pieces in ((6, (own,)), (7, (before,)), (8, (after,)), (9, (far_low, far_high))):
        row = pl.ds(pl.multiple_of(where[at] * rows, rows), rows)
        pieces = [(piece, i) for piece in pieces for i in range(piece.shape[0])]
        for j, (piece, i) in enumerate(pieces):
            out[row, j * cols : (j + 1) * cols] = piece[i]


def per_device(hidden, targets, token_weight, head_weight, *, n_x, n_yl, n_z, n_yh):
    yh, core = lax.axis_index("yh"), lax.axis_index("core")
    tok, width = hidden.shape
    v_dev = head_weight.shape[0]
    half, both, n_own, n_shards = tok // 2, 2 * tok, n_yh * tok, 2 * n_yh

    def local_order(value):
        value = value.reshape(n_yh, 2, tok)
        value = lax.dynamic_slice_in_dim(jnp.concatenate([value, value], 0), yh, n_yh, 0)
        value = jnp.where(core == 0, value, value[:, ::-1])
        return jnp.concatenate([value[0], value[3], value[1], value[2]], 0).reshape(1, -1)

    labels, weights = local_order(targets), local_order(token_weight)
    where = [core, (yh * 2 + core) * v_dev] + [(yh + d) % n_yh for d in (0, n_yh - 1, 1, 2)]
    where = jnp.stack(where + [(lax.axis_index("x") + d) % n_x for d in (0, n_x - 1, 1, 2)])

    smem, vmem = pl.BlockSpec(memory_space=pltpu.SMEM), pl.BlockSpec(memory_space=pltpu.VMEM)
    params = pltpu.CompilerParams(vmem_limit_bytes=16 << 20)
    head_near, own_near = pl.pallas_call(
        stage_kernel,
        out_shape=(jax.ShapeDtypeStruct(head_weight.shape, BF16), jax.ShapeDtypeStruct(hidden.shape, BF16)),
        in_specs=[vmem] * 2,
        out_specs=(vmem,) * 2,
        compiler_params=params,
    )(head_weight, hidden)

    before = shift(hidden, "yh", 1, n_yh)
    after = shift(hidden, "yh", -1, n_yh)
    before, labels, weights, where, head_near, own_near = lax.optimization_barrier(
        (before, labels, weights, where, head_near, own_near)
    )
    far_low = shift(before[:half], "yh", 1, n_yh)
    far_high = shift(after[half:], "yh", -1, n_yh)
    near = (own_near, swap(hidden), before, swap(before), after, swap(after))
    far = (far_low, far_high, swap(far_low), swap(far_high))

    block_logits = jax.ShapeDtypeStruct((v_dev, both), F32)

    *logits, stats = pl.pallas_call(
        logits_kernel,
        out_shape=(block_logits,) * 4 + (jax.ShapeDtypeStruct((n_shards, 8 * n_yh, both), F32),),
        in_specs=[smem] + [vmem] * 12,
        out_specs=(vmem,) * 5,
        compiler_params=params,
        cost_estimate=pl.CostEstimate(
            flops=4 * v_dev * n_own * width,
            bytes_accessed=2 * (v_dev + 2 * n_own) * width,
            transcendentals=2 * v_dev * n_own,
        ),
    )(where, head_near, labels, *near, *far)
    stats = lax.all_to_all(stats, VOCAB, 0, 0, tiled=True)

    cols = min(1024, width)
    whole = lambda *shape: pl.BlockSpec(shape, lambda i: (0,) * len(shape))
    wide = lambda rows: pl.BlockSpec((rows, cols), lambda i: (0, i))
    partial, away, score, loss = pl.pallas_call(
        score_kernel,
        out_shape=(
            jax.ShapeDtypeStruct((v_dev, width), BF16),
            jax.ShapeDtypeStruct((n_own, width), BF16),
            jax.ShapeDtypeStruct((n_own, v_dev), BF16),
            jax.ShapeDtypeStruct((1, both), F32),
        ),
        grid=(width // cols,),
        in_specs=[smem, whole(*stats.shape), whole(1, 2 * n_own), whole(1, 2 * n_own)]
        + [whole(v_dev, both)] * 4
        + [wide(tok)] * 6
        + [wide(half)] * 4
        + [wide(v_dev)],
        out_specs=(wide(v_dev), wide(n_own), whole(n_own, v_dev), whole(1, both)),
        scratch_shapes=[pltpu.VMEM((v_dev, 2 * n_own), BF16), pltpu.VMEM((n_own, v_dev), BF16)],
        compiler_params=params,
        cost_estimate=pl.CostEstimate(
            flops=6 * v_dev * n_own * width,
            bytes_accessed=2 * (2 * v_dev + 3 * n_own) * width,
            transcendentals=2 * v_dev * n_own,
        ),
    )(where, stats, labels, weights, *logits, *near, *far, head_near)
    token_loss = loss[0, :tok]

    part = partial.reshape(n_x, v_dev // n_x, width)
    part = lax.all_to_all(part, "x", 0, 0, tiled=True)

    home = jnp.dot(score, head_near, preferred_element_type=F32).astype(BF16)
    terms = (home.astype(F32) + swap(away).astype(F32)).astype(BF16)
    n_rest, rows = n_yl * n_z, v_dev // n_x
    step = min(4, n_rest)
    part = pl.pallas_call(
        sum_kernel,
        out_shape=jax.ShapeDtypeStruct((n_rest, rows, width // n_rest), BF16),
        grid=(n_rest // step,),
        in_specs=[pl.BlockSpec((n_x, rows, step * width // n_rest), lambda i: (0, 0, i))],
        out_specs=pl.BlockSpec((step, rows, width // n_rest), lambda i: (i, 0, 0)),
        compiler_params=params,
        cost_estimate=pl.CostEstimate(flops=v_dev * width, bytes_accessed=3 * v_dev * width, transcendentals=0),
    )(part)

    mine, up, down, far = (terms[m * tok : (m + 1) * tok] for m in (0, 2, 1, 3))
    from_below = shift(far[:half], "yh", 1, n_yh)
    from_above = shift(far[half:], "yh", -1, n_yh)
    part, from_below, from_above = lax.optimization_barrier((part, from_below, from_above))
    zero = jnp.zeros((half, width), F32)
    up = up.astype(F32) + jnp.concatenate([from_below.astype(F32), zero], 0)
    down = down.astype(F32) + jnp.concatenate([zero, from_above.astype(F32)], 0)
    came = [shift(up.astype(BF16), "yh", 1, n_yh), shift(down.astype(BF16), "yh", -1, n_yh)]

    part = lax.all_to_all(part, ("yl", "z"), 0, 0, tiled=True)
    part = jnp.sum(part.astype(F32), axis=0).astype(BF16)
    part = lax.all_to_all(jnp.broadcast_to(part, (n_yl * n_z,) + part.shape), ("yl", "z"), 0, 0, tiled=True)
    x_before = shift(part, "x", 1, n_x)
    x_after = shift(part, "x", -1, n_x)
    x_low = shift(x_before[: n_rest // 2], "x", 1, n_x)
    x_high = shift(x_after[n_rest // 2 :], "x", -1, n_x)
    grad_weight = pl.pallas_call(
        lay_kernel,
        out_shape=jax.ShapeDtypeStruct((v_dev, width), BF16),
        in_specs=[smem] + [vmem] * 5,
        out_specs=vmem,
        compiler_params=params,
        cost_estimate=pl.CostEstimate(flops=0, bytes_accessed=4 * v_dev * width, transcendentals=0),
    )(where, part, x_before, x_after, x_low, x_high)
    grad_hidden = (mine.astype(F32) + sum(v.astype(F32) for v in came)).astype(BF16)
    return token_loss, grad_hidden, grad_weight


def fine(mesh_devices, sizes):
    mesh = Mesh(mesh_devices.reshape(sizes), ("x", "yl", "z", "yh", "core"))

    def body(*args):
        return per_device(*args, n_x=sizes[0], n_yl=sizes[1], n_z=sizes[2], n_yh=sizes[3])

    tokens = ("x", "yl", "z", "yh", "core")
    return jax.shard_map(
        body,
        mesh=mesh,
        in_specs=(P(tokens, None), P(DP), P(DP), P(VOCAB, None)),
        out_specs=(P(tokens), P(tokens, None), P(VOCAB, None)),
        check_vma=False,
    )


def solution(mesh):
    return fine(mesh.devices, (4, 2, 8, 4, 2))
```

```python
import jax
import jax.numpy as jnp
from jax import lax
from jax.experimental import pallas as pl
from jax.experimental.pallas import tpu as pltpu
from jax.sharding import Mesh
from jax.sharding import PartitionSpec as P

F32, BF16 = jnp.float32, jnp.bfloat16
DP = ("x", "yl", "z")
VOCAB = ("yh", "core")


def shift(value, axis, step, size):
    return lax.ppermute(value, axis, [(i, (i + step) % size) for i in range(size)])


def swap(value):
    return shift(value, "core", 1, 2)


def hits(where, labels, shape):
    return lax.broadcasted_iota(jnp.int32, shape, 0) + where[1] == labels


def block_stats(where, head, pieces, labels, logits):
    rows_t = (((1,), (1,)), ((), ()))
    block = jnp.concatenate([piece[...] for piece in pieces], axis=0)
    value = lax.dot_general(head[...], block, rows_t, preferred_element_type=F32)
    logits[...] = value
    top = jnp.max(value, axis=0, keepdims=True)
    total = jnp.sum(jnp.exp(value - top), axis=0, keepdims=True)
    target = jnp.sum(jnp.where(hits(where, labels, value.shape), value, 0.0), axis=0, keepdims=True)
    blank = jnp.zeros_like(top)
    tile = jnp.concatenate([top, total, target, blank] * 2, axis=0)
    return jnp.where(where[0] == 0, tile, pltpu.roll(tile, tile.shape[1] // 2, 1))


def stage_kernel(head, own, head_out, own_out):
    head_out[...] = head[...]
    own_out[...] = own[...]


def pick(where, tiles, place):
    chosen = tiles[0]
    for m in range(1, 4):
        chosen = jnp.where(where[2 + m] == place, tiles[m], chosen)
    return chosen


def logits_kernel(where, head, labels, *refs):
    pieces, logits, stats = refs[:10], refs[10:14], refs[14]
    n = logits[0].shape[1]
    tiles = []
    for m, chosen in enumerate((pieces[:2], pieces[2:4], pieces[4:6], pieces[6:])):
        tiles.append(block_stats(where, head, chosen, labels[:, m * n : (m + 1) * n], logits[m]))
    upper = lax.broadcasted_iota(jnp.int32, (8, n), 0) < 4
    for pair in range(2):
        line = jnp.where(upper, pick(where, tiles, 2 * pair), pick(where, tiles, 2 * pair + 1))
        for shard in range(stats.shape[0]):
            stats[shard, 8 * pair : 8 * pair + 8, :] = line


def score_kernel(where, stats, labels, weights, *refs):
    all_logits, pieces, head = refs[:4], refs[4:14], refs[14]
    grad, away, score, loss, held, turned, near, sent = refs[15:]
    n = all_logits[0].shape[1]
    half = n // 2

    merged = []
    for place in range(4):
        tops = stats[:, 4 * place, :]
        top = jnp.max(tops, axis=0, keepdims=True)
        total = jnp.sum(stats[:, 4 * place + 1, :] * jnp.exp(tops - top), axis=0, keepdims=True)
        log_total = top + jnp.log(total)
        lost = log_total - jnp.sum(stats[:, 4 * place + 2, :], axis=0, keepdims=True)
        merged.append(jnp.concatenate([log_total, lost] + [jnp.zeros_like(top)] * 6, axis=0))
    for m, logits in enumerate(all_logits):
        lanes = slice(m * n, (m + 1) * n)
        both = merged[0]
        for place in range(1, 4):
            both = jnp.where(where[2 + m] == place, merged[place], both)
        both = jnp.where(where[0] == 0, both, pltpu.roll(both, half, 1))
        if m == 0:
            loss[...] = both[1:2]
        hit = hits(where, labels[:, lanes], logits.shape).astype(F32)
        value = weights[:, lanes] * (jnp.exp(logits[...] - both[0:1]) - hit)
        held[:, lanes] = value.astype(BF16)
        value = value.T.astype(BF16)
        score[m * half : (m + 1) * half] = value[:half]
        turned[m * half : (m + 1) * half] = value[half:]

    cols = head.shape[1] // 4
    copies = []
    for i in range(4):
        span = slice(i * cols, (i + 1) * cols)
        block = jnp.concatenate([piece[:, span] for piece in pieces], axis=0)
        near[:, span] = jnp.dot(held[...], block, preferred_element_type=F32).astype(BF16)
        copies.append(pltpu.make_async_copy(near.at[:, span], grad.at[:, span], sent.at[i]))
        copies[-1].start()
        away[:, span] = jnp.dot(turned[...], head[:, span], preferred_element_type=F32).astype(BF16)
    for copy in copies:
        copy.wait()


def sum_kernel(parts, out):
    cols = out.shape[2]
    for i in range(out.shape[0]):
        part = parts[:, :, i * cols : (i + 1) * cols].astype(F32)
        out[i] = jnp.sum(part, axis=0).astype(BF16)


def lay_kernel(where, own, before, after, far_low, far_high, out):
    n, rows, cols = own.shape
    for at, pieces in ((6, (own,)), (7, (before,)), (8, (after,)), (9, (far_low, far_high))):
        row = pl.ds(pl.multiple_of(where[at] * rows, rows), rows)
        pieces = [(piece, i) for piece in pieces for i in range(piece.shape[0])]
        for j, (piece, i) in enumerate(pieces):
            out[row, j * cols : (j + 1) * cols] = piece[i]


def per_device(hidden, targets, token_weight, head_weight, *, n_x, n_yl, n_z, n_yh):
    yh, core = lax.axis_index("yh"), lax.axis_index("core")
    tok, width = hidden.shape
    v_dev = head_weight.shape[0]
    half, both, n_own, n_shards = tok // 2, 2 * tok, n_yh * tok, 2 * n_yh

    def local_order(value):
        value = value.reshape(n_yh, 2, tok)
        value = lax.dynamic_slice_in_dim(jnp.concatenate([value, value], 0), yh, n_yh, 0)
        value = jnp.where(core == 0, value, value[:, ::-1])
        return jnp.concatenate([value[0], value[3], value[1], value[2]], 0).reshape(1, -1)

    labels, weights = local_order(targets), local_order(token_weight)
    where = [core, (yh * 2 + core) * v_dev] + [(yh + d) % n_yh for d in (0, n_yh - 1, 1, 2)]
    where = jnp.stack(where + [(lax.axis_index("x") + d) % n_x for d in (0, n_x - 1, 1, 2)])

    smem, vmem = pl.BlockSpec(memory_space=pltpu.SMEM), pl.BlockSpec(memory_space=pltpu.VMEM)
    params = pltpu.CompilerParams(vmem_limit_bytes=16 << 20)
    head_near, own_near = pl.pallas_call(
        stage_kernel,
        out_shape=(jax.ShapeDtypeStruct(head_weight.shape, BF16), jax.ShapeDtypeStruct(hidden.shape, BF16)),
        in_specs=[vmem] * 2,
        out_specs=(vmem,) * 2,
        compiler_params=params,
    )(head_weight, hidden)

    before = shift(hidden, "yh", 1, n_yh)
    after = shift(hidden, "yh", -1, n_yh)
    before, labels, weights, where, head_near, own_near = lax.optimization_barrier(
        (before, labels, weights, where, head_near, own_near)
    )
    far_low = shift(before[:half], "yh", 1, n_yh)
    far_high = shift(after[half:], "yh", -1, n_yh)
    near = (own_near, swap(hidden), before, swap(before), after, swap(after))
    far = (far_low, far_high, swap(far_low), swap(far_high))

    block_logits = jax.ShapeDtypeStruct((v_dev, both), F32)

    *logits, stats = pl.pallas_call(
        logits_kernel,
        out_shape=(block_logits,) * 4 + (jax.ShapeDtypeStruct((n_shards, 4 * n_yh, both), F32),),
        in_specs=[smem] + [vmem] * 12,
        out_specs=(vmem,) * 5,
        compiler_params=params,
        cost_estimate=pl.CostEstimate(
            flops=4 * v_dev * n_own * width,
            bytes_accessed=2 * (v_dev + 2 * n_own) * width,
            transcendentals=2 * v_dev * n_own,
        ),
    )(where, head_near, labels, *near, *far)
    stats = lax.all_to_all(stats, VOCAB, 0, 0, tiled=True)

    partial, away, score, loss = pl.pallas_call(
        score_kernel,
        out_shape=(
            jax.ShapeDtypeStruct((v_dev, width), BF16),
            jax.ShapeDtypeStruct((n_own, width), BF16),
            jax.ShapeDtypeStruct((n_own, v_dev), BF16),
            jax.ShapeDtypeStruct((1, both), F32),
        ),
        in_specs=[smem] + [vmem] * 18,
        out_specs=(pl.BlockSpec(memory_space=pl.ANY),) + (vmem,) * 3,
        scratch_shapes=[
            pltpu.VMEM((v_dev, 2 * n_own), BF16),
            pltpu.VMEM((n_own, v_dev), BF16),
            pltpu.VMEM((v_dev, width), BF16),
            pltpu.SemaphoreType.DMA((4,)),
        ],
        compiler_params=pltpu.CompilerParams(vmem_limit_bytes=48 << 20),
        cost_estimate=pl.CostEstimate(
            flops=6 * v_dev * n_own * width,
            bytes_accessed=2 * (2 * v_dev + 3 * n_own) * width,
            transcendentals=2 * v_dev * n_own,
        ),
    )(where, stats, labels, weights, *logits, *near, *far, head_near)
    token_loss = loss[0, :tok]

    part = partial.reshape(n_x, v_dev // n_x, width)
    part = lax.all_to_all(part, "x", 0, 0, tiled=True)

    home = jnp.dot(score, head_near, preferred_element_type=F32).astype(BF16)
    terms = (home.astype(F32) + swap(away).astype(F32)).astype(BF16)
    n_rest, rows = n_yl * n_z, v_dev // n_x
    step = min(4, n_rest)
    part = pl.pallas_call(
        sum_kernel,
        out_shape=jax.ShapeDtypeStruct((n_rest, rows, width // n_rest), BF16),
        grid=(n_rest // step,),
        in_specs=[pl.BlockSpec((n_x, rows, step * width // n_rest), lambda i: (0, 0, i))],
        out_specs=pl.BlockSpec((step, rows, width // n_rest), lambda i: (i, 0, 0)),
        compiler_params=params,
        cost_estimate=pl.CostEstimate(flops=v_dev * width, bytes_accessed=3 * v_dev * width, transcendentals=0),
    )(part)

    mine, up, down, far = (terms[m * tok : (m + 1) * tok] for m in (0, 2, 1, 3))
    from_below = shift(far[:half], "yh", 1, n_yh)
    from_above = shift(far[half:], "yh", -1, n_yh)
    part, from_below, from_above = lax.optimization_barrier((part, from_below, from_above))
    zero = jnp.zeros((half, width), F32)
    up = up.astype(F32) + jnp.concatenate([from_below.astype(F32), zero], 0)
    down = down.astype(F32) + jnp.concatenate([zero, from_above.astype(F32)], 0)
    came = [shift(up.astype(BF16), "yh", 1, n_yh), shift(down.astype(BF16), "yh", -1, n_yh)]

    part = lax.all_to_all(part, ("yl", "z"), 0, 0, tiled=True)
    part = jnp.sum(part.astype(F32), axis=0).astype(BF16)
    part = lax.all_to_all(jnp.broadcast_to(part, (n_yl * n_z,) + part.shape), ("yl", "z"), 0, 0, tiled=True)
    x_before = shift(part, "x", 1, n_x)
    x_after = shift(part, "x", -1, n_x)
    x_low = shift(x_before[: n_rest // 2], "x", 1, n_x)
    x_high = shift(x_after[n_rest // 2 :], "x", -1, n_x)
    grad_weight = pl.pallas_call(
        lay_kernel,
        out_shape=jax.ShapeDtypeStruct((v_dev, width), BF16),
        in_specs=[smem] + [vmem] * 5,
        out_specs=vmem,
        compiler_params=params,
        cost_estimate=pl.CostEstimate(flops=0, bytes_accessed=4 * v_dev * width, transcendentals=0),
    )(where, part, x_before, x_after, x_low, x_high)
    grad_hidden = (mine.astype(F32) + sum(v.astype(F32) for v in came)).astype(BF16)
    return token_loss, grad_hidden, grad_weight


def fine(mesh_devices, sizes):
    mesh = Mesh(mesh_devices.reshape(sizes), ("x", "yl", "z", "yh", "core"))

    def body(*args):
        return per_device(*args, n_x=sizes[0], n_yl=sizes[1], n_z=sizes[2], n_yh=sizes[3])

    tokens = ("x", "yl", "z", "yh", "core")
    return jax.shard_map(
        body,
        mesh=mesh,
        in_specs=(P(tokens, None), P(DP), P(DP), P(VOCAB, None)),
        out_specs=(P(tokens), P(tokens, None), P(VOCAB, None)),
        check_vma=False,
    )


def solution(mesh):
    return fine(mesh.devices, (4, 2, 8, 4, 2))
```

```python
import jax
import jax.numpy as jnp
from jax import lax
from jax.experimental import pallas as pl
from jax.experimental.pallas import tpu as pltpu
from jax.sharding import Mesh
from jax.sharding import PartitionSpec as P

F32, BF16 = jnp.float32, jnp.bfloat16
DP = ("x", "yl", "z")
VOCAB = ("yh", "core")


def shift(value, axis, step, size):
    return lax.ppermute(value, axis, [(i, (i + step) % size) for i in range(size)])


def swap(value):
    return shift(value, "core", 1, 2)


def hits(where, labels, shape):
    return lax.broadcasted_iota(jnp.int32, shape, 0) + where[1] == labels


def block_stats(where, head, pieces, labels, logits):
    rows_t = (((1,), (1,)), ((), ()))
    block = jnp.concatenate([piece[...] for piece in pieces], axis=0)
    value = lax.dot_general(head[...], block, rows_t, preferred_element_type=F32)
    logits[...] = value
    top = jnp.max(value, axis=0, keepdims=True)
    total = jnp.sum(jnp.exp(value - top), axis=0, keepdims=True)
    target = jnp.sum(jnp.where(hits(where, labels, value.shape), value, 0.0), axis=0, keepdims=True)
    blank = jnp.zeros_like(top)
    tile = jnp.concatenate([top, total, target, blank] * 2, axis=0)
    return jnp.where(where[0] == 0, tile, pltpu.roll(tile, tile.shape[1] // 2, 1))


def stage_kernel(head, own, head_out, own_out):
    head_out[...] = head[...]
    own_out[...] = own[...]


def pick(where, tiles, place):
    chosen = tiles[0]
    for m in range(1, 4):
        chosen = jnp.where(where[2 + m] == place, tiles[m], chosen)
    return chosen


def logits_kernel(where, head, labels, *refs):
    pieces, logits, stats = refs[:10], refs[10:14], refs[14]
    n = logits[0].shape[1]
    tiles = []
    for m, chosen in enumerate((pieces[:2], pieces[2:4], pieces[4:6], pieces[6:])):
        tiles.append(block_stats(where, head, chosen, labels[:, m * n : (m + 1) * n], logits[m]))
    upper = lax.broadcasted_iota(jnp.int32, (8, n), 0) < 4
    for pair in range(2):
        line = jnp.where(upper, pick(where, tiles, 2 * pair), pick(where, tiles, 2 * pair + 1))
        for shard in range(stats.shape[0]):
            stats[shard, 8 * pair : 8 * pair + 8, :] = line


def score_kernel(where, stats, labels, weights, *refs):
    all_logits, pieces, head = refs[:4], refs[4:14], refs[14]
    grad, away, score, loss, held, turned, near, sent = refs[15:]
    n = all_logits[0].shape[1]
    half = n // 2

    merged = []
    for place in range(4):
        tops = stats[:, 4 * place, :]
        top = jnp.max(tops, axis=0, keepdims=True)
        total = jnp.sum(stats[:, 4 * place + 1, :] * jnp.exp(tops - top), axis=0, keepdims=True)
        log_total = top + jnp.log(total)
        lost = log_total - jnp.sum(stats[:, 4 * place + 2, :], axis=0, keepdims=True)
        merged.append(jnp.concatenate([log_total, lost] + [jnp.zeros_like(top)] * 6, axis=0))
    for m, logits in enumerate(all_logits):
        lanes = slice(m * n, (m + 1) * n)
        both = merged[0]
        for place in range(1, 4):
            both = jnp.where(where[2 + m] == place, merged[place], both)
        both = jnp.where(where[0] == 0, both, pltpu.roll(both, half, 1))
        if m == 0:
            loss[...] = both[1:2]
        hit = hits(where, labels[:, lanes], logits.shape).astype(F32)
        value = weights[:, lanes] * (jnp.exp(logits[...] - both[0:1]) - hit)
        held[:, lanes] = value.astype(BF16)
        value = value.T.astype(BF16)
        score[m * half : (m + 1) * half] = value[:half]
        turned[m * half : (m + 1) * half] = value[half:]

    cols = head.shape[1] // 4
    copies = []
    for i in range(4):
        span = slice(i * cols, (i + 1) * cols)
        block = jnp.concatenate([piece[:, span] for piece in pieces], axis=0)
        near[:, span] = jnp.dot(held[...], block, preferred_element_type=F32).astype(BF16)
        copies.append(pltpu.make_async_copy(near.at[:, span], grad.at[:, span], sent.at[i]))
        copies[-1].start()
        away[:, span] = jnp.dot(turned[...], head[:, span], preferred_element_type=F32).astype(BF16)
    for copy in copies:
        copy.wait()


def sum_kernel(parts, out):
    cols = out.shape[2]
    for i in range(out.shape[0]):
        part = parts[:, :, i * cols : (i + 1) * cols].astype(F32)
        out[i] = jnp.sum(part, axis=0).astype(BF16)


def lay_kernel(where, own, before, after, far_low, far_high, out):
    n, rows, cols = own.shape
    for at, pieces in ((6, (own,)), (7, (before,)), (8, (after,)), (9, (far_low, far_high))):
        row = pl.ds(pl.multiple_of(where[at] * rows, rows), rows)
        pieces = [(piece, i) for piece in pieces for i in range(piece.shape[0])]
        for j, (piece, i) in enumerate(pieces):
            out[row, j * cols : (j + 1) * cols] = piece[i]


def per_device(hidden, targets, token_weight, head_weight, *, n_x, n_yl, n_z, n_yh):
    yh, core = lax.axis_index("yh"), lax.axis_index("core")
    tok, width = hidden.shape
    v_dev = head_weight.shape[0]
    half, both, n_own, n_shards = tok // 2, 2 * tok, n_yh * tok, 2 * n_yh

    def local_order(value):
        value = value.reshape(n_yh, 2, tok)
        value = lax.dynamic_slice_in_dim(jnp.concatenate([value, value], 0), yh, n_yh, 0)
        value = jnp.where(core == 0, value, value[:, ::-1])
        return jnp.concatenate([value[0], value[3], value[1], value[2]], 0).reshape(1, -1)

    labels, weights = local_order(targets), local_order(token_weight)
    where = [core, (yh * 2 + core) * v_dev] + [(yh + d) % n_yh for d in (0, n_yh - 1, 1, 2)]
    where = jnp.stack(where + [(lax.axis_index("x") + d) % n_x for d in (0, n_x - 1, 1, 2)])

    smem, vmem = pl.BlockSpec(memory_space=pltpu.SMEM), pl.BlockSpec(memory_space=pltpu.VMEM)
    params = pltpu.CompilerParams(vmem_limit_bytes=16 << 20)
    head_near, own_near = pl.pallas_call(
        stage_kernel,
        out_shape=(jax.ShapeDtypeStruct(head_weight.shape, BF16), jax.ShapeDtypeStruct(hidden.shape, BF16)),
        in_specs=[vmem] * 2,
        out_specs=(vmem,) * 2,
        compiler_params=params,
    )(head_weight, hidden)

    before = shift(hidden, "yh", 1, n_yh)
    after = shift(hidden, "yh", -1, n_yh)
    before, labels, weights, where, head_near, own_near = lax.optimization_barrier(
        (before, labels, weights, where, head_near, own_near)
    )
    far_low = shift(before[:half], "yh", 1, n_yh)
    far_high = shift(after[half:], "yh", -1, n_yh)
    near = (own_near, swap(hidden), before, swap(before), after, swap(after))
    far = (far_low, far_high, swap(far_low), swap(far_high))

    block_logits = jax.ShapeDtypeStruct((v_dev, both), F32)

    *logits, stats = pl.pallas_call(
        logits_kernel,
        out_shape=(block_logits,) * 4 + (jax.ShapeDtypeStruct((n_shards, 4 * n_yh, both), F32),),
        in_specs=[smem] + [vmem] * 12,
        out_specs=(vmem,) * 5,
        compiler_params=params,
        cost_estimate=pl.CostEstimate(
            flops=4 * v_dev * n_own * width,
            bytes_accessed=2 * (v_dev + 2 * n_own) * width,
            transcendentals=2 * v_dev * n_own,
        ),
    )(where, head_near, labels, *near, *far)
    stats = lax.all_to_all(stats, VOCAB, 0, 0, tiled=True)

    partial, away, score, loss = pl.pallas_call(
        score_kernel,
        out_shape=(
            jax.ShapeDtypeStruct((v_dev, width), BF16),
            jax.ShapeDtypeStruct((n_own, width), BF16),
            jax.ShapeDtypeStruct((n_own, v_dev), BF16),
            jax.ShapeDtypeStruct((1, both), F32),
        ),
        in_specs=[smem] + [vmem] * 18,
        out_specs=(pl.BlockSpec(memory_space=pl.ANY),) + (vmem,) * 3,
        scratch_shapes=[
            pltpu.VMEM((v_dev, 2 * n_own), BF16),
            pltpu.VMEM((n_own, v_dev), BF16),
            pltpu.VMEM((v_dev, width), BF16),
            pltpu.SemaphoreType.DMA((4,)),
        ],
        compiler_params=pltpu.CompilerParams(vmem_limit_bytes=48 << 20),
        cost_estimate=pl.CostEstimate(
            flops=6 * v_dev * n_own * width,
            bytes_accessed=2 * (2 * v_dev + 3 * n_own) * width,
            transcendentals=2 * v_dev * n_own,
        ),
    )(where, stats, labels, weights, *logits, *near, *far, head_near)
    token_loss = loss[0, :tok]

    part = partial.reshape(n_x, v_dev // n_x, width)
    part = lax.all_to_all(part, "x", 0, 0, tiled=True)

    home = jnp.dot(score, head_near, preferred_element_type=F32).astype(BF16)
    terms = (home.astype(F32) + swap(away).astype(F32)).astype(BF16)
    n_rest, rows = n_yl * n_z, v_dev // n_x
    step = min(4, n_rest)
    part = pl.pallas_call(
        sum_kernel,
        out_shape=jax.ShapeDtypeStruct((n_rest, rows, width // n_rest), BF16),
        grid=(n_rest // step,),
        in_specs=[pl.BlockSpec((n_x, rows, step * width // n_rest), lambda i: (0, 0, i))],
        out_specs=pl.BlockSpec((step, rows, width // n_rest), lambda i: (i, 0, 0)),
        compiler_params=params,
        cost_estimate=pl.CostEstimate(flops=v_dev * width, bytes_accessed=3 * v_dev * width, transcendentals=0),
    )(part)

    mine, up, down, far = (terms[m * tok : (m + 1) * tok] for m in (0, 2, 1, 3))
    from_below = shift(far[:half], "yh", 1, n_yh)
    from_above = shift(far[half:], "yh", -1, n_yh)
    part, from_below, from_above = lax.optimization_barrier((part, from_below, from_above))
    up_high = shift(up[half:], "yh", 1, n_yh)
    down_low = shift(down[:half], "yh", -1, n_yh)
    up_low = (up[:half].astype(F32) + from_below.astype(F32)).astype(BF16)
    down_high = (down[half:].astype(F32) + from_above.astype(F32)).astype(BF16)
    up_low, down_high = shift(up_low, "yh", 1, n_yh), shift(down_high, "yh", -1, n_yh)

    part = lax.all_to_all(part, ("yl", "z"), 0, 0, tiled=True)
    part, up_high, down_low = lax.optimization_barrier((part, up_high, down_low))
    part = jnp.sum(part.astype(F32), axis=0).astype(BF16)
    part = lax.all_to_all(jnp.broadcast_to(part, (n_yl * n_z,) + part.shape), ("yl", "z"), 0, 0, tiled=True)
    part, up_low, down_high = lax.optimization_barrier((part, up_low, down_high))
    x_before = shift(part, "x", 1, n_x)
    x_after = shift(part, "x", -1, n_x)
    x_low = shift(x_before[: n_rest // 2], "x", 1, n_x)
    x_high = shift(x_after[n_rest // 2 :], "x", -1, n_x)
    grad_weight = pl.pallas_call(
        lay_kernel,
        out_shape=jax.ShapeDtypeStruct((v_dev, width), BF16),
        in_specs=[smem] + [vmem] * 5,
        out_specs=vmem,
        compiler_params=params,
        cost_estimate=pl.CostEstimate(flops=0, bytes_accessed=4 * v_dev * width, transcendentals=0),
    )(where, part, x_before, x_after, x_low, x_high)
    came = jnp.concatenate([up_low, up_high], 0), jnp.concatenate([down_low, down_high], 0)
    grad_hidden = (mine.astype(F32) + sum(v.astype(F32) for v in came)).astype(BF16)
    return token_loss, grad_hidden, grad_weight


def fine(mesh_devices, sizes):
    mesh = Mesh(mesh_devices.reshape(sizes), ("x", "yl", "z", "yh", "core"))

    def body(*args):
        return per_device(*args, n_x=sizes[0], n_yl=sizes[1], n_z=sizes[2], n_yh=sizes[3])

    tokens = ("x", "yl", "z", "yh", "core")
    return jax.shard_map(
        body,
        mesh=mesh,
        in_specs=(P(tokens, None), P(DP), P(DP), P(VOCAB, None)),
        out_specs=(P(tokens), P(tokens, None), P(VOCAB, None)),
        check_vma=False,
    )


def solution(mesh):
    return fine(mesh.devices, (4, 2, 8, 4, 2))
```

```python
import jax
import jax.numpy as jnp
from jax import lax
from jax.experimental import pallas as pl
from jax.experimental.pallas import tpu as pltpu
from jax.sharding import Mesh
from jax.sharding import PartitionSpec as P

F32, BF16 = jnp.float32, jnp.bfloat16
DP = ("x", "yl", "z")
VOCAB = ("yh", "core")


def shift(value, axis, step, size):
    return lax.ppermute(value, axis, [(i, (i + step) % size) for i in range(size)])


def swap(value):
    return shift(value, "core", 1, 2)


def hits(where, labels, shape):
    return lax.broadcasted_iota(jnp.int32, shape, 0) + where[1] == labels


def block_stats(where, head, pieces, labels, logits):
    rows_t = (((1,), (1,)), ((), ()))
    block = jnp.concatenate([piece[...] for piece in pieces], axis=0)
    value = lax.dot_general(head[...], block, rows_t, preferred_element_type=F32)
    logits[...] = value
    top = jnp.max(value, axis=0, keepdims=True)
    total = jnp.sum(jnp.exp(value - top), axis=0, keepdims=True)
    target = jnp.sum(jnp.where(hits(where, labels, value.shape), value, 0.0), axis=0, keepdims=True)
    blank = jnp.zeros_like(top)
    tile = jnp.concatenate([top, total, target, blank] * 2, axis=0)
    return jnp.where(where[0] == 0, tile, pltpu.roll(tile, tile.shape[1] // 2, 1))


def stage_kernel(head, own, head_out, own_out):
    head_out[...] = head[...]
    own_out[...] = own[...]


def pick(where, tiles, place):
    chosen = tiles[0]
    for m in range(1, 4):
        chosen = jnp.where(where[2 + m] == place, tiles[m], chosen)
    return chosen


def logits_kernel(where, head, labels, *refs):
    pieces, logits, stats = refs[:10], refs[10:14], refs[14]
    n = logits[0].shape[1]
    tiles = []
    for m, chosen in enumerate((pieces[:2], pieces[2:4], pieces[4:6], pieces[6:])):
        tiles.append(block_stats(where, head, chosen, labels[:, m * n : (m + 1) * n], logits[m]))
    upper = lax.broadcasted_iota(jnp.int32, (8, n), 0) < 4
    for pair in range(2):
        line = jnp.where(upper, pick(where, tiles, 2 * pair), pick(where, tiles, 2 * pair + 1))
        for shard in range(stats.shape[0]):
            stats[shard, 8 * pair : 8 * pair + 8, :] = line


def score_kernel(where, stats, labels, weights, *refs):
    all_logits, pieces, head = refs[:4], refs[4:14], refs[14]
    grad, away, score, loss, held, turned, near, sent = refs[15:]
    n = all_logits[0].shape[1]
    half = n // 2

    merged = []
    for place in range(4):
        tops = stats[:, 4 * place, :]
        top = jnp.max(tops, axis=0, keepdims=True)
        total = jnp.sum(stats[:, 4 * place + 1, :] * jnp.exp(tops - top), axis=0, keepdims=True)
        log_total = top + jnp.log(total)
        lost = log_total - jnp.sum(stats[:, 4 * place + 2, :], axis=0, keepdims=True)
        merged.append(jnp.concatenate([log_total, lost] + [jnp.zeros_like(top)] * 6, axis=0))
    for m, logits in enumerate(all_logits):
        lanes = slice(m * n, (m + 1) * n)
        both = merged[0]
        for place in range(1, 4):
            both = jnp.where(where[2 + m] == place, merged[place], both)
        both = jnp.where(where[0] == 0, both, pltpu.roll(both, half, 1))
        if m == 0:
            loss[...] = both[1:2]
        hit = hits(where, labels[:, lanes], logits.shape).astype(F32)
        value = weights[:, lanes] * (jnp.exp(logits[...] - both[0:1]) - hit)
        held[:, lanes] = value.astype(BF16)
        value = value.T.astype(BF16)
        score[m * half : (m + 1) * half] = value[:half]
        turned[m * half : (m + 1) * half] = value[half:]

    cols = head.shape[1] // 4
    copies = []
    for i in range(4):
        span = slice(i * cols, (i + 1) * cols)
        block = jnp.concatenate([piece[:, span] for piece in pieces], axis=0)
        near[:, span] = jnp.dot(held[...], block, preferred_element_type=F32).astype(BF16)
        copies.append(pltpu.make_async_copy(near.at[:, span], grad.at[:, span], sent.at[i]))
        copies[-1].start()
        away[:, span] = jnp.dot(turned[...], head[:, span], preferred_element_type=F32).astype(BF16)
    for copy in copies:
        copy.wait()


def sum_kernel(parts, out):
    cols = out.shape[2]
    for i in range(out.shape[0]):
        part = parts[:, :, i * cols : (i + 1) * cols].astype(F32)
        out[i] = jnp.sum(part, axis=0).astype(BF16)


def lay_kernel(pieces, out):
    cols = pieces.shape[3]
    for i in range(pieces.shape[1]):
        out[:, i * cols : (i + 1) * cols] = pieces[0, i]


def per_device(hidden, targets, token_weight, head_weight, *, n_x, n_yl, n_z, n_yh):
    yh, core = lax.axis_index("yh"), lax.axis_index("core")
    tok, width = hidden.shape
    v_dev = head_weight.shape[0]
    half, both, n_own, n_shards = tok // 2, 2 * tok, n_yh * tok, 2 * n_yh

    def local_order(value):
        value = value.reshape(n_yh, 2, tok)
        value = lax.dynamic_slice_in_dim(jnp.concatenate([value, value], 0), yh, n_yh, 0)
        value = jnp.where(core == 0, value, value[:, ::-1])
        return jnp.concatenate([value[0], value[3], value[1], value[2]], 0).reshape(1, -1)

    labels, weights = local_order(targets), local_order(token_weight)
    where = [core, (yh * 2 + core) * v_dev] + [(yh + d) % n_yh for d in (0, n_yh - 1, 1, 2)]
    where = jnp.stack(where)

    smem, vmem = pl.BlockSpec(memory_space=pltpu.SMEM), pl.BlockSpec(memory_space=pltpu.VMEM)
    params = pltpu.CompilerParams(vmem_limit_bytes=16 << 20)
    head_near, own_near = pl.pallas_call(
        stage_kernel,
        out_shape=(jax.ShapeDtypeStruct(head_weight.shape, BF16), jax.ShapeDtypeStruct(hidden.shape, BF16)),
        in_specs=[vmem] * 2,
        out_specs=(vmem,) * 2,
        compiler_params=params,
    )(head_weight, hidden)

    before = shift(hidden, "yh", 1, n_yh)
    after = shift(hidden, "yh", -1, n_yh)
    before, labels, weights, where, head_near, own_near = lax.optimization_barrier(
        (before, labels, weights, where, head_near, own_near)
    )
    far_low = shift(before[:half], "yh", 1, n_yh)
    far_high = shift(after[half:], "yh", -1, n_yh)
    near = (own_near, swap(hidden), before, swap(before), after, swap(after))
    far = (far_low, far_high, swap(far_low), swap(far_high))

    block_logits = jax.ShapeDtypeStruct((v_dev, both), F32)

    *logits, stats = pl.pallas_call(
        logits_kernel,
        out_shape=(block_logits,) * 4 + (jax.ShapeDtypeStruct((n_shards, 4 * n_yh, both), F32),),
        in_specs=[smem] + [vmem] * 12,
        out_specs=(vmem,) * 5,
        compiler_params=params,
        cost_estimate=pl.CostEstimate(
            flops=4 * v_dev * n_own * width,
            bytes_accessed=2 * (v_dev + 2 * n_own) * width,
            transcendentals=2 * v_dev * n_own,
        ),
    )(where, head_near, labels, *near, *far)
    stats = lax.all_to_all(stats, VOCAB, 0, 0, tiled=True)

    partial, away, score, loss = pl.pallas_call(
        score_kernel,
        out_shape=(
            jax.ShapeDtypeStruct((v_dev, width), BF16),
            jax.ShapeDtypeStruct((n_own, width), BF16),
            jax.ShapeDtypeStruct((n_own, v_dev), BF16),
            jax.ShapeDtypeStruct((1, both), F32),
        ),
        in_specs=[smem] + [vmem] * 18,
        out_specs=(pl.BlockSpec(memory_space=pl.ANY),) + (vmem,) * 3,
        scratch_shapes=[
            pltpu.VMEM((v_dev, 2 * n_own), BF16),
            pltpu.VMEM((n_own, v_dev), BF16),
            pltpu.VMEM((v_dev, width), BF16),
            pltpu.SemaphoreType.DMA((4,)),
        ],
        compiler_params=pltpu.CompilerParams(vmem_limit_bytes=48 << 20),
        cost_estimate=pl.CostEstimate(
            flops=6 * v_dev * n_own * width,
            bytes_accessed=2 * (2 * v_dev + 3 * n_own) * width,
            transcendentals=2 * v_dev * n_own,
        ),
    )(where, stats, labels, weights, *logits, *near, *far, head_near)
    token_loss = loss[0, :tok]

    part = partial.reshape(n_x, v_dev // n_x, width)
    part = lax.all_to_all(part, "x", 0, 0, tiled=True)

    home = jnp.dot(score, head_near, preferred_element_type=F32).astype(BF16)
    terms = (home.astype(F32) + swap(away).astype(F32)).astype(BF16)
    n_rest, rows = n_yl * n_z, v_dev // n_x
    step = min(4, n_rest)
    part = pl.pallas_call(
        sum_kernel,
        out_shape=jax.ShapeDtypeStruct((n_rest, rows, width // n_rest), BF16),
        grid=(n_rest // step,),
        in_specs=[pl.BlockSpec((n_x, rows, step * width // n_rest), lambda i: (0, 0, i))],
        out_specs=pl.BlockSpec((step, rows, width // n_rest), lambda i: (i, 0, 0)),
        compiler_params=params,
        cost_estimate=pl.CostEstimate(flops=v_dev * width, bytes_accessed=3 * v_dev * width, transcendentals=0),
    )(part)

    mine, up, down, far = (terms[m * tok : (m + 1) * tok] for m in (0, 2, 1, 3))
    from_below = shift(far[:half], "yh", 1, n_yh)
    from_above = shift(far[half:], "yh", -1, n_yh)
    part, from_below, from_above = lax.optimization_barrier((part, from_below, from_above))
    zero = jnp.zeros((half, width), F32)
    up = up.astype(F32) + jnp.concatenate([from_below.astype(F32), zero], 0)
    down = down.astype(F32) + jnp.concatenate([zero, from_above.astype(F32)], 0)
    came = [shift(up.astype(BF16), "yh", 1, n_yh), shift(down.astype(BF16), "yh", -1, n_yh)]

    part = lax.all_to_all(part, ("yl", "z"), 0, 0, tiled=True)
    part = jnp.sum(part.astype(F32), axis=0).astype(BF16)
    part = lax.all_to_all(jnp.broadcast_to(part, (n_x * n_rest,) + part.shape), DP, 0, 0, tiled=True)
    part = part.reshape((n_x, n_rest) + part.shape[1:])
    grad_weight = pl.pallas_call(
        lay_kernel,
        out_shape=jax.ShapeDtypeStruct((v_dev, width), BF16),
        grid=(n_x,),
        in_specs=[pl.BlockSpec((1,) + part.shape[1:], lambda i: (i, 0, 0, 0))],
        out_specs=pl.BlockSpec((rows, width), lambda i: (i, 0)),
        compiler_params=params,
        cost_estimate=pl.CostEstimate(flops=0, bytes_accessed=4 * v_dev * width, transcendentals=0),
    )(part)
    grad_hidden = (mine.astype(F32) + sum(v.astype(F32) for v in came)).astype(BF16)
    return token_loss, grad_hidden, grad_weight


def fine(mesh_devices, sizes):
    mesh = Mesh(mesh_devices.reshape(sizes), ("x", "yl", "z", "yh", "core"))

    def body(*args):
        return per_device(*args, n_x=sizes[0], n_yl=sizes[1], n_z=sizes[2], n_yh=sizes[3])

    tokens = ("x", "yl", "z", "yh", "core")
    return jax.shard_map(
        body,
        mesh=mesh,
        in_specs=(P(tokens, None), P(DP), P(DP), P(VOCAB, None)),
        out_specs=(P(tokens), P(tokens, None), P(VOCAB, None)),
        check_vma=False,
    )


def solution(mesh):
    return fine(mesh.devices, (4, 2, 8, 4, 2))
```

```python
import jax
import jax.numpy as jnp
from jax import lax
from jax.experimental import pallas as pl
from jax.experimental.pallas import tpu as pltpu
from jax.sharding import Mesh
from jax.sharding import PartitionSpec as P

F32, BF16 = jnp.float32, jnp.bfloat16
DP = ("x", "yl", "z")
VOCAB = ("yh", "core")


def shift(value, axis, step, size):
    return lax.ppermute(value, axis, [(i, (i + step) % size) for i in range(size)])


def swap(value):
    return shift(value, "core", 1, 2)


def hits(where, labels, shape):
    return lax.broadcasted_iota(jnp.int32, shape, 0) + where[1] == labels


def block_stats(where, head, pieces, labels, logits):
    rows_t = (((1,), (1,)), ((), ()))
    block = jnp.concatenate([piece[...] for piece in pieces], axis=0)
    value = lax.dot_general(head[...], block, rows_t, preferred_element_type=F32)
    logits[...] = value
    top = jnp.max(value, axis=0, keepdims=True)
    total = jnp.sum(jnp.exp(value - top), axis=0, keepdims=True)
    target = jnp.sum(jnp.where(hits(where, labels, value.shape), value, 0.0), axis=0, keepdims=True)
    blank = jnp.zeros_like(top)
    tile = jnp.concatenate([top, total, target, blank] * 2, axis=0)
    return jnp.where(where[0] == 0, tile, pltpu.roll(tile, tile.shape[1] // 2, 1))


def stage_kernel(head, own, head_out, own_out):
    head_out[...] = head[...]
    own_out[...] = own[...]


def pick(where, tiles, place):
    chosen = tiles[0]
    for m in range(1, 4):
        chosen = jnp.where(where[2 + m] == place, tiles[m], chosen)
    return chosen


def logits_kernel(where, head, labels, *refs):
    pieces, logits, stats = refs[:10], refs[10:14], refs[14]
    n = logits[0].shape[1]
    tiles = []
    for m, chosen in enumerate((pieces[:2], pieces[2:4], pieces[4:6], pieces[6:])):
        tiles.append(block_stats(where, head, chosen, labels[:, m * n : (m + 1) * n], logits[m]))
    upper = lax.broadcasted_iota(jnp.int32, (8, n), 0) < 4
    for pair in range(2):
        line = jnp.where(upper, pick(where, tiles, 2 * pair), pick(where, tiles, 2 * pair + 1))
        for shard in range(stats.shape[0]):
            stats[shard, 8 * pair : 8 * pair + 8, :] = line


def score_kernel(where, stats, labels, weights, *refs):
    all_logits, pieces, head = refs[:4], refs[4:14], refs[14]
    grad, away, score, loss, held, turned, near, sent = refs[15:]
    n = all_logits[0].shape[1]
    half = n // 2

    merged = []
    for place in range(4):
        tops = stats[:, 4 * place, :]
        top = jnp.max(tops, axis=0, keepdims=True)
        total = jnp.sum(stats[:, 4 * place + 1, :] * jnp.exp(tops - top), axis=0, keepdims=True)
        log_total = top + jnp.log(total)
        lost = log_total - jnp.sum(stats[:, 4 * place + 2, :], axis=0, keepdims=True)
        merged.append(jnp.concatenate([log_total, lost] + [jnp.zeros_like(top)] * 6, axis=0))
    for m, logits in enumerate(all_logits):
        lanes = slice(m * n, (m + 1) * n)
        both = merged[0]
        for place in range(1, 4):
            both = jnp.where(where[2 + m] == place, merged[place], both)
        both = jnp.where(where[0] == 0, both, pltpu.roll(both, half, 1))
        if m == 0:
            loss[...] = both[1:2]
        hit = hits(where, labels[:, lanes], logits.shape).astype(F32)
        value = weights[:, lanes] * (jnp.exp(logits[...] - both[0:1]) - hit)
        held[:, lanes] = value.astype(BF16)
        value = value.T.astype(BF16)
        score[m * half : (m + 1) * half] = value[:half]
        turned[m * half : (m + 1) * half] = value[half:]

    cols = head.shape[1] // 4
    copies = []
    for i in range(4):
        span = slice(i * cols, (i + 1) * cols)
        block = jnp.concatenate([piece[:, span] for piece in pieces], axis=0)
        near[:, span] = jnp.dot(held[...], block, preferred_element_type=F32).astype(BF16)
        copies.append(pltpu.make_async_copy(near.at[:, span], grad.at[:, span], sent.at[i]))
        copies[-1].start()
        away[:, span] = jnp.dot(turned[...], head[:, span], preferred_element_type=F32).astype(BF16)
    for copy in copies:
        copy.wait()


def sum_kernel(parts, out):
    cols = out.shape[2]
    for i in range(out.shape[0]):
        part = parts[:, :, i * cols : (i + 1) * cols].astype(F32)
        out[i] = jnp.sum(part, axis=0).astype(BF16)


def lay_kernel(pieces, out):
    cols = pieces.shape[3]
    for i in range(pieces.shape[1]):
        out[:, i * cols : (i + 1) * cols] = pieces[0, i]


def per_device(hidden, targets, token_weight, head_weight, *, n_x, n_yl, n_z, n_yh):
    yh, core = lax.axis_index("yh"), lax.axis_index("core")
    tok, width = hidden.shape
    v_dev = head_weight.shape[0]
    half, both, n_own, n_shards = tok // 2, 2 * tok, n_yh * tok, 2 * n_yh

    def local_order(value):
        value = value.reshape(n_yh, 2, tok)
        value = lax.dynamic_slice_in_dim(jnp.concatenate([value, value], 0), yh, n_yh, 0)
        value = jnp.where(core == 0, value, value[:, ::-1])
        return jnp.concatenate([value[0], value[3], value[1], value[2]], 0).reshape(1, -1)

    labels, weights = local_order(targets), local_order(token_weight)
    where = [core, (yh * 2 + core) * v_dev] + [(yh + d) % n_yh for d in (0, n_yh - 1, 1, 2)]
    where = jnp.stack(where)

    smem, vmem = pl.BlockSpec(memory_space=pltpu.SMEM), pl.BlockSpec(memory_space=pltpu.VMEM)
    params = pltpu.CompilerParams(vmem_limit_bytes=16 << 20)
    head_near, own_near = pl.pallas_call(
        stage_kernel,
        out_shape=(jax.ShapeDtypeStruct(head_weight.shape, BF16), jax.ShapeDtypeStruct(hidden.shape, BF16)),
        in_specs=[vmem] * 2,
        out_specs=(vmem,) * 2,
        compiler_params=params,
    )(head_weight, hidden)

    before = shift(hidden, "yh", 1, n_yh)
    after = shift(hidden, "yh", -1, n_yh)
    before, labels, weights, where, head_near, own_near = lax.optimization_barrier(
        (before, labels, weights, where, head_near, own_near)
    )
    far_low = shift(before[:half], "yh", 1, n_yh)
    far_high = shift(after[half:], "yh", -1, n_yh)
    near = (own_near, swap(hidden), before, swap(before), after, swap(after))
    far = (far_low, far_high, swap(far_low), swap(far_high))

    block_logits = jax.ShapeDtypeStruct((v_dev, both), F32)

    *logits, stats = pl.pallas_call(
        logits_kernel,
        out_shape=(block_logits,) * 4 + (jax.ShapeDtypeStruct((n_shards, 4 * n_yh, both), F32),),
        in_specs=[smem] + [vmem] * 12,
        out_specs=(vmem,) * 5,
        compiler_params=params,
        cost_estimate=pl.CostEstimate(
            flops=4 * v_dev * n_own * width,
            bytes_accessed=2 * (v_dev + 2 * n_own) * width,
            transcendentals=2 * v_dev * n_own,
        ),
    )(where, head_near, labels, *near, *far)
    stats = lax.all_to_all(stats, VOCAB, 0, 0, tiled=True)

    partial, away, score, loss = pl.pallas_call(
        score_kernel,
        out_shape=(
            jax.ShapeDtypeStruct((v_dev, width), BF16),
            jax.ShapeDtypeStruct((n_own, width), BF16),
            jax.ShapeDtypeStruct((n_own, v_dev), BF16),
            jax.ShapeDtypeStruct((1, both), F32),
        ),
        in_specs=[smem] + [vmem] * 18,
        out_specs=(pl.BlockSpec(memory_space=pl.ANY),) + (vmem,) * 3,
        scratch_shapes=[
            pltpu.VMEM((v_dev, 2 * n_own), BF16),
            pltpu.VMEM((n_own, v_dev), BF16),
            pltpu.VMEM((v_dev, width), BF16),
            pltpu.SemaphoreType.DMA((4,)),
        ],
        compiler_params=pltpu.CompilerParams(vmem_limit_bytes=48 << 20),
        cost_estimate=pl.CostEstimate(
            flops=6 * v_dev * n_own * width,
            bytes_accessed=2 * (2 * v_dev + 3 * n_own) * width,
            transcendentals=2 * v_dev * n_own,
        ),
    )(where, stats, labels, weights, *logits, *near, *far, head_near)
    token_loss = loss[0, :tok]

    part = partial.reshape(n_x, v_dev // n_x, width)
    part = lax.all_to_all(part, "x", 0, 0, tiled=True)

    home = jnp.dot(score, head_near, preferred_element_type=F32).astype(BF16)
    terms = (home.astype(F32) + swap(away).astype(F32)).astype(BF16)
    n_rest, rows = n_yl * n_z, v_dev // n_x
    step = min(4, n_rest)
    part = pl.pallas_call(
        sum_kernel,
        out_shape=jax.ShapeDtypeStruct((n_rest, rows, width // n_rest), BF16),
        grid=(n_rest // step,),
        in_specs=[pl.BlockSpec((n_x, rows, step * width // n_rest), lambda i: (0, 0, i))],
        out_specs=pl.BlockSpec((step, rows, width // n_rest), lambda i: (i, 0, 0)),
        compiler_params=params,
        cost_estimate=pl.CostEstimate(flops=v_dev * width, bytes_accessed=3 * v_dev * width, transcendentals=0),
    )(part)

    mine, up, down, far = (terms[m * tok : (m + 1) * tok] for m in (0, 2, 1, 3))
    from_below = shift(far[:half], "yh", 1, n_yh)
    from_above = shift(far[half:], "yh", -1, n_yh)
    part, from_below, from_above = lax.optimization_barrier((part, from_below, from_above))
    zero = jnp.zeros((half, width), F32)
    up = up.astype(F32) + jnp.concatenate([from_below.astype(F32), zero], 0)
    down = down.astype(F32) + jnp.concatenate([zero, from_above.astype(F32)], 0)
    came = [shift(up.astype(BF16), "yh", 1, n_yh), shift(down.astype(BF16), "yh", -1, n_yh)]

    part = lax.all_to_all(part, ("yl", "z"), 0, 0, tiled=True)
    part = jnp.sum(part.astype(F32), axis=0).astype(BF16)
    part = lax.all_to_all(jnp.broadcast_to(part, (n_rest,) + part.shape), ("yl", "z"), 0, 0, tiled=True)
    part = lax.all_to_all(jnp.broadcast_to(part, (n_x,) + part.shape), "x", 0, 0, tiled=True)
    grad_weight = pl.pallas_call(
        lay_kernel,
        out_shape=jax.ShapeDtypeStruct((v_dev, width), BF16),
        grid=(n_x,),
        in_specs=[pl.BlockSpec((1,) + part.shape[1:], lambda i: (i, 0, 0, 0))],
        out_specs=pl.BlockSpec((rows, width), lambda i: (i, 0)),
        compiler_params=params,
        cost_estimate=pl.CostEstimate(flops=0, bytes_accessed=4 * v_dev * width, transcendentals=0),
    )(part)
    grad_hidden = (mine.astype(F32) + sum(v.astype(F32) for v in came)).astype(BF16)
    return token_loss, grad_hidden, grad_weight


def fine(mesh_devices, sizes):
    mesh = Mesh(mesh_devices.reshape(sizes), ("x", "yl", "z", "yh", "core"))

    def body(*args):
        return per_device(*args, n_x=sizes[0], n_yl=sizes[1], n_z=sizes[2], n_yh=sizes[3])

    tokens = ("x", "yl", "z", "yh", "core")
    return jax.shard_map(
        body,
        mesh=mesh,
        in_specs=(P(tokens, None), P(DP), P(DP), P(VOCAB, None)),
        out_specs=(P(tokens), P(tokens, None), P(VOCAB, None)),
        check_vma=False,
    )


def solution(mesh):
    return fine(mesh.devices, (4, 2, 8, 4, 2))
```
